32 devices in a mesh: dp: 8 (over y, x, core), tensor: 4 (over z).
Axes of the slice: x: 2, y: 2, z: 4, core: 2. Of those that a mesh axis runs over, the one named last changes fastest.
Arguments:
- layer_input: float32 [8192, 1536], P(('dp', 'tensor')), may hold values from -6 to 6
- segment_ids: int32 [8192], P('dp'), may hold values from 0 to 23, as said below
- attn_gain: float32 [1536], replicated, may hold values from 0.25 to 1.75
- query_weight: float32 [1536, 1536], P('dp', 'tensor'), may hold values from -0.15625 to 0.15625
- key_weight: float32 [1536, 1536], P('dp', 'tensor'), may hold values from -0.15625 to 0.15625
- value_weight: float32 [1536, 1536], P('dp', 'tensor'), may hold values from -0.15625 to 0.15625
- forget_weight: float32 [1536, 24], P('dp', 'tensor'), may hold values from -0.15625 to 0.15625
- forget_bias: float32 [24], replicated, may hold values from 0 to 6
- output_weight: float32 [1536, 1536], P('dp', 'tensor'), may hold values from -0.4375 to 0.4375
- feed_gain: float32 [1536], replicated, may hold values from 0.25 to 1.75
- gate_weight: float32 [1536, 4096], P('dp', 'tensor'), may hold values from -0.15625 to 0.15625
- up_weight: float32 [1536, 4096], P('dp', 'tensor'), may hold values from -0.15625 to 0.15625
- down_weight: float32 [1536, 4096], P('dp', 'tensor'), may hold values from -0.1875 to 0.1875
- output_cotangent: float32 [8192, 1536], P(('dp', 'tensor')), may hold values from -6 to 6
Outputs:
- layer_output: float32 [8192, 1536], P(('dp', 'tensor'))
- input_grad: float32 [8192, 1536], P(('dp', 'tensor'))
- attn_gain_grad: float32 [1536], replicated
- query_grad: float32 [1536, 1536], P('dp', 'tensor')
- key_grad: float32 [1536, 1536], P('dp', 'tensor')
- value_grad: float32 [1536, 1536], P('dp', 'tensor')
- forget_grad: float32 [1536, 24], P('dp', 'tensor')
- bias_grad: float32 [24], replicated
- output_grad: float32 [1536, 1536], P('dp', 'tensor')
- feed_gain_grad: float32 [1536], replicated
- gate_grad: float32 [1536, 4096], P('dp', 'tensor')
- up_grad: float32 [1536, 4096], P('dp', 'tensor')
- down_grad: float32 [1536, 4096], P('dp', 'tensor')
The draws below stay inside these ranges and needn't reach their ends.
Inputs may be any that keep to these rules, and one draw needn't show every extreme that they name: `segment_ids`: each sequence of 1024 tokens holds three documents and begins a new number; numbers never fall and rise by one at each document start. The middle document has exactly 800 tokens, the first 60 to 164 tokens, the last the rest.
All inputs are finite; a program needn't handle non-finite values.
Results may differ from the reference program's by a relative error of at most 0.014.
Values may be sent and summed in bfloat16 or wider, within the bound.
No kernel may reach another device: no remote copies, remote signals or barrier semaphores. Data moves between devices by JAX's collectives and lax.ppermute only.
A program may use at most 192 MiB of HBM per device.

```python
import math
import jax
import jax.numpy as jnp
from jax import lax

D = 1536
H = 24
DH = 64
FF = 4096
LEN = 1024
TOKENS = 8192
LONG_DOC = 800
SHORT_LEAST = 60


def draw_segment_ids(key, part):
    key = jax.random.fold_in(key, 11)
    sequences = TOKENS // LEN
    starts = jax.random.randint(key, (sequences,), SHORT_LEAST, LEN - LONG_DOC - SHORT_LEAST + 1)
    place = jnp.arange(TOKENS, dtype=jnp.int32)
    which = place // LEN
    offset = place % LEN
    begin = starts[which]
    local = (offset >= begin).astype(jnp.int32) + (offset >= begin + LONG_DOC).astype(jnp.int32)
    return (3 * which + local).astype(jnp.int32)


def raised(values, key, source, target, parts, factor):
    def block_of(dim):
        return (jnp.arange(values.shape[dim]) // (values.shape[dim] // parts)).reshape((-1,) + (1,) * (values.ndim - 1 - dim))

    near = jax.random.permutation(key, parts)[block_of(target)]
    far = (block_of(target) + parts // 2) % parts
    return jnp.where((block_of(source) == near) | (block_of(source) == far), factor * values, values)


def block_levels(rng, extent, cuts, least, largest):
    level = 1.0
    for dim, parts in cuts:
        heights = jax.random.uniform(jax.random.fold_in(jax.random.fold_in(rng, 6), dim), (parts,), jnp.float32, least / len(cuts), largest / len(cuts))
        level = level * jnp.repeat(jnp.exp(heights), extent[dim] // parts).reshape((-1,) + (1,) * (len(extent) - 1 - dim))
    return level


def gaussian(own_key, extent, scale, most, shards=(), kind=jnp.bfloat16):
    factor_of = block_levels(own_key, extent, shards, -0.22, 0.18) if shards else 1.0
    array = jax.random.normal(own_key, extent, jnp.float32) * scale * factor_of
    return jnp.minimum(jnp.maximum(array, -most), most).astype(kind)


def noise_with(stream_key, dims, deviation, limit, split, heavy, kind=jnp.bfloat16):
    values = deviation * jax.random.normal(stream_key, dims, jnp.float32)
    if split:
        values = values * block_levels(stream_key, dims, split, -0.22, 0.18)
    return jnp.clip(raised(values, jax.random.fold_in(stream_key, 3), *heavy), -limit, limit).astype(kind)


def setup_inputs(seed: int = 0) -> dict:
    streams_of = jax.random.split(jax.random.key(seed), 15)
    layer_input = noise_with(streams_of[0], (TOKENS, D), 1.0, 6.0, ((0, 32),), (0, 1, 32, 2.75), jnp.float32)
    segment_ids = draw_segment_ids(jax.random.fold_in(streams_of[14], 71), 0)
    attn_gain = jnp.clip(1.0 + 0.15 * jax.random.normal(streams_of[2], (D,), jnp.float32), 0.25, 1.75)
    query_weight = gaussian(streams_of[3], (D, D), D ** -0.5, 0.15625, ((0, 8), (1, 4)), jnp.float32)
    key_weight = gaussian(streams_of[4], (D, D), D ** -0.5, 0.15625, ((0, 8), (1, 4)), jnp.float32)
    value_weight = gaussian(streams_of[5], (D, D), D ** -0.5, 0.15625, ((0, 8), (1, 4)), jnp.float32)
    forget_weight = gaussian(streams_of[6], (D, H), D ** -0.5, 0.15625, ((0, 8), (1, 4)), jnp.float32)
    forget_bias = jnp.clip(jax.random.uniform(streams_of[7], (H,), jnp.float32, 0.0, 6.0), 0.0, 6.0)
    output_weight = gaussian(streams_of[8], (D, D), (D // 8) ** -0.5, 0.4375, ((0, 8), (1, 4)), jnp.float32)
    feed_gain = jnp.clip(1.0 + 0.15 * jax.random.normal(streams_of[9], (D,), jnp.float32), 0.25, 1.75)
    gate_weight = gaussian(streams_of[10], (D, FF), D ** -0.5, 0.15625, ((0, 8), (1, 4)), jnp.float32)
    up_weight = gaussian(streams_of[11], (D, FF), D ** -0.5, 0.15625, ((0, 8), (1, 4)), jnp.float32)
    down_weight = gaussian(streams_of[12], (D, FF), (FF // 4) ** -0.5, 0.1875, ((0, 8), (1, 4)), jnp.float32)
    output_cotangent = noise_with(streams_of[13], (TOKENS, D), 1.0, 6.0, ((0, 32),), (0, 1, 32, 2.75), jnp.float32)
    return dict(layer_input=layer_input, segment_ids=segment_ids, attn_gain=attn_gain, query_weight=query_weight, key_weight=key_weight, value_weight=value_weight, forget_weight=forget_weight, forget_bias=forget_bias, output_weight=output_weight, feed_gain=feed_gain, gate_weight=gate_weight, up_weight=up_weight, down_weight=down_weight, output_cotangent=output_cotangent)


@jax.custom_vjp
def low(v):
    return lax.optimization_barrier(v.astype(jnp.bfloat16)).astype(jnp.float32)

@jax.custom_vjp
def low_back(v):
    return v

def low_keep(v):
    return (low(v), None)

def low_pass(kept, grad):
    return (grad,)

def back_keep(v):
    return (v, None)

def back_low(kept, grad):
    return (low(grad),)
low.defvjp(low_keep, low_pass)
low_back.defvjp(back_keep, back_low)

def product(left, right):
    return jnp.dot(left, right, precision=lax.Precision.HIGHEST)

def product_t(left, right):
    return jnp.dot(left, right.T, precision=lax.Precision.HIGHEST)

def norm_rows(rows, gain):
    return rows * lax.rsqrt(lax.optimization_barrier(jnp.mean(rows * rows, axis=-1, keepdims=True)) + 1e-06) * gain

def attend(pack):
    queries, keys, values, decays, segment = pack
    scale = DH ** (-0.5)
    raw = low_back(jnp.einsum('hid,hjd->hij', queries, keys, precision=lax.Precision.HIGHEST))
    scores = raw * scale + decays[:, :, None] - decays[:, None, :]
    place = jnp.arange(LEN, dtype=jnp.int32)
    allowed = (place[None, :] <= place[:, None]) & (segment[:, None] == segment[None, :])
    scores = jnp.where(allowed[None], scores, -1e+30)
    highest = lax.optimization_barrier(jnp.max(scores, axis=-1, keepdims=True))
    powers = jnp.exp(scores - highest)
    shares = powers / lax.optimization_barrier(jnp.sum(powers, axis=-1, keepdims=True))
    mixed = jnp.einsum('hij,hjd->hid', low(shares), values, precision=lax.Precision.HIGHEST)
    return low(low_back(mixed))

def forward(rows, segment_ids, attn_gain, query_weight, key_weight, value_weight, forget_weight, forget_bias, output_weight, feed_gain, gate_weight, up_weight, down_weight):
    sequences = rows.shape[0] // LEN
    attn_normed = low(norm_rows(rows, attn_gain))
    queries = low(low_back(product(attn_normed, low(query_weight))))
    keys = low(low_back(product(attn_normed, low(key_weight))))
    values = low(low_back(product(attn_normed, low(value_weight))))
    logits = low_back(product(attn_normed, low(forget_weight)) + forget_bias)
    logdecay = -jax.nn.softplus(-logits)
    cumdecay = jnp.cumsum(logdecay.reshape(sequences, LEN, H), axis=1)

    def split_heads(tensor):
        return tensor.reshape(sequences, LEN, H, DH).transpose(0, 2, 1, 3)
    mixed = lax.map(jax.checkpoint(attend), (split_heads(queries), split_heads(keys), split_heads(values), cumdecay.transpose(0, 2, 1), segment_ids.reshape(sequences, LEN)))
    mixed = mixed.transpose(0, 2, 1, 3).reshape(sequences * LEN, D)
    middle = rows + low_back(product_t(mixed, low(output_weight)))
    feed_normed = low(norm_rows(middle, feed_gain))
    gate = low_back(product(feed_normed, low(gate_weight)))
    up = low_back(product(feed_normed, low(up_weight)))
    hidden = low(jax.nn.silu(gate) * up)
    return middle + low_back(product_t(hidden, low(down_weight)))

def reference(layer_input, segment_ids, attn_gain, query_weight, key_weight, value_weight, forget_weight, forget_bias, output_weight, feed_gain, gate_weight, up_weight, down_weight, output_cotangent):
    sequences = TOKENS // LEN
    group = math.gcd(sequences, max(1, 4096 // LEN))
    groups = sequences // group
    weights = (attn_gain, query_weight, key_weight, value_weight, forget_weight, forget_bias, output_weight, feed_gain, gate_weight, up_weight, down_weight)
    inputs = layer_input.reshape(groups, group * LEN, D)
    segments = segment_ids.reshape(groups, group * LEN)
    cotangents = output_cotangent.reshape(groups, group * LEN, D)

    def step(totals, pack):
        rows, segment, cotangent = pack

        def run(rows_in, *params):
            return forward(rows_in, segment, *params)
        result, pullback = jax.vjp(run, rows, *weights)
        grads = pullback(cotangent)
        totals = tuple((total + grad for total, grad in zip(totals, grads[1:])))
        return (totals, (result, grads[0]))
    zeros = tuple((jnp.zeros_like(weight) for weight in weights))
    totals, (results, input_grads) = lax.scan(step, zeros, (inputs, segments, cotangents))
    return (results.reshape(TOKENS, D), input_grads.reshape(TOKENS, D), totals[0], totals[1], totals[2], totals[3], totals[4], totals[5], totals[6], totals[7], totals[8], totals[9], totals[10])
```

```python
import functools

import jax
import jax.numpy as jnp
from jax import lax
from jax.experimental import pallas as pl
from jax.experimental.pallas import tpu as pltpu
from jax.sharding import PartitionSpec as P

F32 = jnp.float32
BF = jnp.bfloat16
NT = (((1,), (1,)), ((), ()))
NN = (((1,), (0,)), ((), ()))
TN = (((0,), (0,)), ((), ()))
BOTH = ("dp", "tensor")
EPS = 1e-6


def dotf(a, b, dn):
    return lax.dot_general(a, b, dn, preferred_element_type=F32)


def split3(x):
    a=x.astype(BF); r=x-a.astype(F32); b=r.astype(BF); c=(r-b.astype(F32)).astype(BF)
    return a,b,c

def fwd_kernel(heads, qb, x_ref, logit_ref, segc_ref, segr_ref, mixed_ref, rows_ref, dcol_ref, lse_sc, drow_sc):
    T=x_ref.shape[0]; W=heads*64
    logits=logit_ref[...]
    ld=-(jnp.maximum(-logits,0.0)+jnp.log1p(jnp.exp(-jnp.abs(logits))))
    ri=lax.broadcasted_iota(jnp.int32,(128,128),0); ci=lax.broadcasted_iota(jnp.int32,(128,128),1)
    tri=(ri>=ci).astype(BF)
    carry=jnp.zeros((1,128),F32)
    for b in range(T//128):
        blk=ld[b*128:(b+1)*128]
        a,bb,c=split3(blk)
        pre=dotf(tri,a,NN)+dotf(tri,bb,NN)+dotf(tri,c,NN)+carry
        dcol_ref[b*128:(b+1)*128,:]=pre
        drow_sc[:,b*128:(b+1)*128]=pre.T
        carry=pre[127:128]
    lane=lax.broadcasted_iota(jnp.int32,(1,128),1)
    rq=lax.broadcasted_iota(jnp.int32,(qb,qb),0); cq=lax.broadcasted_iota(jnp.int32,(qb,qb),1)
    causal=rq>=cq
    for pr in range(heads//2):
        c0=pr*128
        for b in range(T//qb):
            r0=b*qb; L=r0+qb
            q=x_ref[r0:L,c0:c0+128].astype(F32)*0.125
            k=x_ref[0:L,W+c0:W+c0+128]
            v=x_ref[0:L,2*W+c0:2*W+c0+128]
            same=segc_ref[r0:L,:]==segr_ref[:,0:L]
            outs=[]
            for hh in range(2):
                h=2*pr+hh
                qm=jnp.where((lane>=64) if hh else (lane<64),q,0.0).astype(BF)
                s=dotf(qm,k,NT)
                s=s+dcol_ref[r0:L,h:h+1]-drow_sc[h:h+1,0:L]
                s=jnp.where(same,s,-1e30)
                sd=jnp.where(causal,s[:,r0:],-1e30)
                s=sd if b==0 else jnp.concatenate([s[:,:r0],sd],axis=1)
                m=jnp.max(s,axis=1,keepdims=True)
                p=jnp.exp(s-m)
                l=jnp.sum(p,axis=1,keepdims=True)
                o=dotf(p.astype(BF),v,NN)/l
                outs.append(o)
                lse_sc[r0:L,h:h+1]=m+jnp.log(l)
            mixed_ref[r0:L,c0:c0+128]=jnp.where(lane<64,outs[0],outs[1]).astype(BF)
    rows_ref[0:8,:]=drow_sc[0:8,:]
    for b in range(T//128):
        rows_ref[8:16,b*128:(b+1)*128]=lse_sc[b*128:(b+1)*128,:].T[0:8]

def attn_fwd(qkv, logits, segc, segr, heads=6, qb=256):
    T=qkv.shape[0]
    return pl.pallas_call(functools.partial(fwd_kernel,heads,qb),
        out_shape=(jax.ShapeDtypeStruct((T,heads*64),BF),jax.ShapeDtypeStruct((16,T),F32),jax.ShapeDtypeStruct((T,128),F32)),
        scratch_shapes=[pltpu.VMEM((T,128),F32),pltpu.VMEM((128,T),F32)],
        compiler_params=pltpu.CompilerParams(vmem_limit_bytes=60*1024*1024),
        cost_estimate=pl.CostEstimate(flops=3*10**9,bytes_accessed=4*10**6,transcendentals=4*10**6),
        name="attend_fwd")(qkv,logits,segc,segr)

def bwd_kernel(heads, kb, x_ref, mixed_ref, mb_ref, rows_ref, dcol_ref, segc_ref, segr_ref, grad_ref, drow_ref, dq_sc, rs_sc):
    T=x_ref.shape[0]; W=heads*64
    lane=lax.broadcasted_iota(jnp.int32,(1,128),1)
    rq=lax.broadcasted_iota(jnp.int32,(kb,kb),0); cq=lax.broadcasted_iota(jnp.int32,(kb,kb),1)
    causal=rq<=cq
    for pr in range(heads//2):
        c0=pr*128
        prod=mb_ref[:,c0:c0+128].astype(F32)*mixed_ref[:,c0:c0+128].astype(F32)
        rr=lax.broadcasted_iota(jnp.int32,(8,128),0); ll=lax.broadcasted_iota(jnp.int32,(8,128),1)
        sel=((ll//64)==rr).astype(BF)
        a,b_,c_=split3(prod)
        delta=dotf(sel,a,NT)+dotf(sel,b_,NT)+dotf(sel,c_,NT)
        for b in range(T//kb):
            k0=b*kb
            k=x_ref[k0:k0+kb,W+c0:W+c0+128]
            v=x_ref[k0:k0+kb,2*W+c0:2*W+c0+128]
            q=x_ref[k0:T,c0:c0+128]
            do=mb_ref[k0:T,c0:c0+128]
            same=segc_ref[k0:k0+kb,:]==segr_ref[:,k0:T]
            dks=[];dvs=[];dqs=[]
            for hh in range(2):
                h=2*pr+hh
                msk=(lane>=64) if hh else (lane<64)
                km=jnp.where(msk,k.astype(F32)*0.125,0.0).astype(BF)
                vm=jnp.where(msk,v.astype(F32),0.0).astype(BF)
                s=dotf(km,q,NT)
                r=rows_ref[h:h+1,k0:T]-rows_ref[8+h:9+h,k0:T]
                s=s+r-dcol_ref[k0:k0+kb,h:h+1]
                s=jnp.where(same,s,-1e30)
                sd=jnp.where(causal,s[:,:kb],-1e30)
                s=sd if k0+kb==T else jnp.concatenate([sd,s[:,kb:]],axis=1)
                p=jnp.exp(s)
                dvs.append(dotf(p.astype(BF),do,NN))
                dp=dotf(vm,do,NT)
                ds=p*(dp-delta[hh:hh+1,k0:T])
                dsl=(ds*0.125).astype(BF)
                dks.append(dotf(dsl,q,NN))
                dqs.append(dotf(dsl,k,TN))
                cs=jnp.sum(ds,axis=1,keepdims=True)
                rs_=jnp.sum(ds,axis=0,keepdims=True)
                rs_sc[k0:k0+kb,h:h+1]=cs
                if b==0: drow_ref[h:h+1,:]=rs_
                else: drow_ref[h:h+1,k0:T]+=rs_
            grad_ref[k0:k0+kb,W+c0:W+c0+128]=jnp.where(lane<64,dks[0],dks[1]).astype(BF)
            grad_ref[k0:k0+kb,2*W+c0:2*W+c0+128]=jnp.where(lane<64,dvs[0],dvs[1]).astype(BF)
            dq=jnp.where(lane<64,dqs[0],dqs[1])
            if b==0: dq_sc[...]=dq
            else: dq_sc[k0:T,:]+=dq
        grad_ref[:,c0:c0+128]=dq_sc[...].astype(BF)
    for b in range(T//128):
        drow_ref[:,b*128:(b+1)*128]=drow_ref[:,b*128:(b+1)*128]-rs_sc[b*128:(b+1)*128,:].T[0:8]

def attn_bwd(qkv, mixed, mb, rows, dcol, segc, segr, heads=6, kb=256):
    T=qkv.shape[0]
    return pl.pallas_call(functools.partial(bwd_kernel,heads,kb),
        out_shape=(jax.ShapeDtypeStruct((T,3*heads*64),BF),jax.ShapeDtypeStruct((8,T),F32)),
        scratch_shapes=[pltpu.VMEM((T,128),F32),pltpu.VMEM((T,128),F32)],
        compiler_params=pltpu.CompilerParams(vmem_limit_bytes=60*1024*1024),
        cost_estimate=pl.CostEstimate(flops=8*10**9,bytes_accessed=8*10**6,transcendentals=4*10**6),
        name="attend_bwd")(qkv,mixed,mb,rows,dcol,segc,segr)


class Layout:
    def __init__(self, dp, tensor):
        self.groups = [[core + 2 * i for i in range(dp // 2)] for core in range(2)]
        self.core = [(d, d ^ 1) for d in range(dp)]
        self.pair = [(z, z ^ 1) for z in range(tensor)]
        flat = lambda d, z: d * tensor + z
        devices = [(d, z) for d in range(dp) for z in range(tensor)]
        away = [(d, z) for d, z in devices if (d & 1) != (z >> 1)]
        near = [(d, z) for d, z in devices if (d & 1) == (z >> 1)]
        self.move = [(flat(d, z), flat(d ^ 1, z ^ 2)) for d, z in away]
        self.pair_near = [(flat(d, z), flat(d, z ^ 1)) for d, z in near]
        self.pair_away = [(flat(d, z), flat(d, z ^ 1)) for d, z in away]
        even = [(d, z) for d, z in devices if d & 1 == 0]
        odd = [(d, z) for d, z in devices if d & 1 == 1]
        self.even_far = [(flat(d, z), flat(d + 1, z ^ 2)) for d, z in even]
        self.odd_far = [(flat(d, z), flat(d, z ^ 2)) for d, z in odd]
        self.odd_even = [(flat(d, z), flat(d - 1, z)) for d, z in odd]
        self.back_even_far = [(b, a) for a, b in self.even_far]
        self.back_odd_even = [(b, a) for a, b in self.odd_even]


def cat(*parts):
    return jnp.concatenate(parts, axis=0)


def gather_weight(lay, w, odd):
    a = lax.ppermute(w, BOTH, lay.even_far)
    b = lax.ppermute(w, BOTH, lay.odd_far)
    c = lax.ppermute(w, BOTH, lay.odd_even)
    rows = jnp.where(odd, cat(a, b), cat(w, c))
    return lax.all_gather(rows, "dp", axis=0, tiled=True, axis_index_groups=lay.groups)


def scatter_grad(lay, g, odd):
    r = lax.psum_scatter(
        g, "dp", scatter_dimension=0, tiled=True, axis_index_groups=lay.groups
    )
    half = r.shape[0] // 2
    low, high = r[:half], r[half:]
    a = lax.ppermute(low, BOTH, lay.back_even_far)
    b = lax.ppermute(high, BOTH, lay.odd_far)
    c = lax.ppermute(high, BOTH, lay.back_odd_even)
    return jnp.where(odd, c, low).astype(F32) + jnp.where(odd, b, a).astype(F32)


def gather_pair(lay, x):
    z = lax.ppermute(x, "tensor", lay.pair)
    near = cat(x, z)
    return cat(near, lax.ppermute(near, "dp", lay.core))


def scatter_pair(lay, part):
    half = part.shape[0] // 2
    quarter = half // 2
    got = lax.ppermute(part[half:], "dp", lay.core)
    mine = part[:half].astype(F32) + got.astype(F32)
    got = lax.ppermute(mine[quarter:].astype(BF), "tensor", lay.pair)
    return mine[:quarter] + got.astype(F32)


def gather_sequence(lay, x, odd, zodd, away):
    moved = lax.ppermute(x, BOTH, lay.move)
    near = lax.ppermute(x, BOTH, lay.pair_near)
    far = lax.ppermute(moved, BOTH, lay.pair_away)
    mine = jnp.where(away, moved, x)
    other = jnp.where(away, far, near)
    half = jnp.where(zodd, cat(other, mine), cat(mine, other))
    got = lax.ppermute(half, "dp", lay.core)
    return jnp.where(odd, cat(got, half), cat(half, got))


def scatter_sequence(lay, part, odd, zodd, away):
    half = part.shape[0] // 2
    quarter = half // 2
    first, second = part[:half], part[half:]
    got = lax.ppermute(jnp.where(odd, first, second), "dp", lay.core)
    mine = jnp.where(odd, second, first).astype(F32) + got.astype(F32)
    first, second = mine[:quarter], mine[quarter:]
    got = lax.ppermute(jnp.where(zodd, first, second).astype(BF), "tensor", lay.pair)
    mine = jnp.where(zodd, second, first) + got.astype(F32)
    got = lax.ppermute(mine.astype(BF), BOTH, lay.move)
    return jnp.where(away, got.astype(F32), mine)


def inverse_rms(rows):
    return lax.rsqrt(jnp.mean(rows * rows, axis=-1, keepdims=True) + EPS)


def norm_back(rows, gain, grad):
    r = inverse_rms(rows)
    xhat = rows * r
    scaled = grad * gain
    back = r * (scaled - xhat * jnp.mean(scaled * xhat, axis=-1, keepdims=True))
    return back, jnp.sum(grad * xhat, axis=0)


def per_device(
    layer_input,
    segment_ids,
    attn_gain,
    query_weight,
    key_weight,
    value_weight,
    forget_weight,
    forget_bias,
    output_weight,
    feed_gain,
    gate_weight,
    up_weight,
    down_weight,
    output_cotangent,
):
    lay = Layout(lax.axis_size("dp"), lax.axis_size("tensor"))
    z = lax.axis_index("tensor")
    odd = (lax.axis_index("dp") & 1) == 1
    zodd = (z & 1) == 1
    away = odd != (z >= 2)
    quarter = jnp.where(odd, z ^ 2, z)
    heads = forget_weight.shape[1]
    width = query_weight.shape[1]
    hidden_width = gate_weight.shape[1]
    forget_pad = jnp.pad(forget_weight, ((0, 0), (0, 128 - heads)))

    normed = (layer_input * inverse_rms(layer_input) * attn_gain).astype(BF)
    w_attn_local = jnp.concatenate(
        [query_weight, key_weight, value_weight, forget_pad, output_weight], axis=1
    ).astype(BF)
    w_feed_local = jnp.concatenate([gate_weight, up_weight, down_weight], axis=1).astype(BF)
    w_attn = gather_weight(lay, w_attn_local, odd)
    w_feed = gather_weight(lay, w_feed_local, odd)
    w_qkv = w_attn[:, : 3 * width]
    w_forget = w_attn[:, 3 * width : 3 * width + 128]
    w_output = w_attn[:, 3 * width + 128 :]
    w_gate = w_feed[:, :hidden_width]
    w_up = w_feed[:, hidden_width : 2 * hidden_width]
    w_down = w_feed[:, 2 * hidden_width :]

    segment = jnp.where(away, lax.ppermute(segment_ids, "dp", lay.core), segment_ids)
    bias = jnp.pad(
        lax.dynamic_slice_in_dim(forget_bias, quarter * heads, heads), (0, 128 - heads)
    )

    attn_normed = gather_sequence(lay, normed, odd, zodd, away)
    qkv = dotf(attn_normed, w_qkv, NN).astype(BF)
    logits = dotf(attn_normed, w_forget, NN) + bias
    segc, segr = segment[:, None], segment[None, :]
    mixed, rows, dcol = attn_fwd(qkv, logits, segc, segr, heads)
    branch = scatter_sequence(lay, dotf(mixed, w_output, NT).astype(BF), odd, zodd, away)
    middle = layer_input + branch

    feed_normed = gather_pair(lay, (middle * inverse_rms(middle) * feed_gain).astype(BF))
    cot_low = gather_pair(lay, output_cotangent.astype(BF))
    gate = dotf(feed_normed, w_gate, NN)
    up = dotf(feed_normed, w_up, NN)
    sig = jax.nn.sigmoid(gate)
    silu = gate * sig
    hidden = (silu * up).astype(BF)
    hidden_grad = dotf(cot_low, w_down, NN)
    gate_back = (hidden_grad * up * sig * (1.0 + gate * (1.0 - sig))).astype(BF)
    up_back = (hidden_grad * silu).astype(BF)
    feed_part = (dotf(gate_back, w_gate, NT) + dotf(up_back, w_up, NT)).astype(BF)
    feed_normed_grad = scatter_pair(lay, feed_part)
    layer_output = middle + scatter_pair(lay, dotf(hidden, w_down, NT).astype(BF))
    feed_grads = jnp.concatenate(
        [
            dotf(feed_normed, gate_back, TN).astype(BF),
            dotf(feed_normed, up_back, TN).astype(BF),
            dotf(cot_low, hidden, TN).astype(BF),
        ],
        axis=1,
    )
    feed_shard = scatter_grad(lay, feed_grads, odd)

    middle_part, feed_gain_part = norm_back(middle, feed_gain, feed_normed_grad)
    middle_grad = output_cotangent + middle_part
    middle_low = gather_sequence(lay, middle_grad.astype(BF), odd, zodd, away)
    mixed_back = dotf(middle_low, w_output, NN).astype(BF)
    grads, decay_grad = attn_bwd(qkv, mixed, mixed_back, rows, dcol, segc, segr, heads)
    later = jnp.dot(
        decay_grad,
        jnp.tril(jnp.ones((decay_grad.shape[1],) * 2, F32)),
        precision=lax.Precision.HIGHEST,
    )
    logit_back = (jnp.pad(later.T, ((0, 0), (0, 120))) * jax.nn.sigmoid(-logits)).astype(BF)
    lane = jnp.arange(128)[None, :]
    logit_back = jnp.where(lane < heads, logit_back, 0)
    attn_part = (
        dotf(grads, w_qkv, NT) + dotf(logit_back, w_forget, NT)
    ).astype(BF)
    attn_normed_grad = scatter_sequence(lay, attn_part, odd, zodd, away)
    attn_grads = jnp.concatenate(
        [
            dotf(attn_normed, grads, TN).astype(BF),
            dotf(attn_normed, logit_back, TN).astype(BF),
            dotf(middle_low, mixed, TN).astype(BF),
        ],
        axis=1,
    )
    attn_shard = scatter_grad(lay, attn_grads, odd)
    input_part, attn_gain_part = norm_back(layer_input, attn_gain, attn_normed_grad)
    input_grad = middle_grad + input_part

    bias_part = jnp.sum(logit_back[:, :heads].astype(F32), axis=0)
    bias_full = lax.dynamic_update_slice_in_dim(
        jnp.zeros(forget_bias.shape, F32), bias_part, quarter * heads, 0
    )
    n = attn_gain.shape[0]
    small = lax.psum(cat(attn_gain_part, feed_gain_part, bias_full), BOTH)
    return (
        layer_output,
        input_grad,
        small[:n],
        attn_shard[:, :width],
        attn_shard[:, width : 2 * width],
        attn_shard[:, 2 * width : 3 * width],
        attn_shard[:, 3 * width : 3 * width + heads],
        small[2 * n :],
        attn_shard[:, 3 * width + 128 :],
        small[n : 2 * n],
        feed_shard[:, :hidden_width],
        feed_shard[:, hidden_width : 2 * hidden_width],
        feed_shard[:, 2 * hidden_width :],
    )


def solution(mesh):
    tokens = P(("dp", "tensor"), None)
    weight = P("dp", "tensor")
    in_specs = (
        tokens, P("dp"), P(), weight, weight, weight, weight, P(), weight, P(), weight, weight, weight, tokens,
    )
    out_specs = (
        tokens, tokens, P(), weight, weight, weight, weight, P(), weight, P(), weight, weight, weight,
    )
    return jax.shard_map(
        per_device, mesh=mesh, in_specs=in_specs, out_specs=out_specs, check_vma=False
    )
```

```python
import functools

import jax
import jax.numpy as jnp
from jax import lax
from jax.experimental import pallas as pl
from jax.experimental.pallas import tpu as pltpu
from jax.sharding import PartitionSpec as P

F32 = jnp.float32
BF = jnp.bfloat16
NT = (((1,), (1,)), ((), ()))
NN = (((1,), (0,)), ((), ()))
TN = (((0,), (0,)), ((), ()))
BOTH = ("dp", "tensor")
EPS = 1e-6


def dotf(a, b, dn):
    return lax.dot_general(a, b, dn, preferred_element_type=F32)


VMEM_LIMIT = 60 * 1024 * 1024


def split3(x):
    a = x.astype(BF)
    r = x - a.astype(F32)
    b = r.astype(BF)
    return a, b, (r - b.astype(F32)).astype(BF)


def exact_dot(left, right, dims):
    return sum(dotf(left, part, dims) for part in split3(right))


def column_of(row):
    parts = [
        jnp.broadcast_to(row[:, i : i + 128], (128, 128)).T[:, :1]
        for i in range(0, row.shape[1], 128)
    ]
    return jnp.concatenate(parts, axis=0)


def attend_kernel(
    heads, span, x_ref, w_ref, bias_ref, seg_ref, qkv_ref, mixed_ref, branch_ref, rows_ref, decay_ref, closed_ref, stat_ref, drow_ref
):
    length = x_ref.shape[0]
    width = heads * 64
    x = x_ref[...]
    qkv_ref[...] = dotf(x, w_ref[:, : 3 * width], NN).astype(BF)
    logits = dotf(x, w_ref[:, 3 * width : 3 * width + 128], NN) + bias_ref[...]
    small = jnp.exp(-jnp.abs(logits))
    log_decay = -(jnp.maximum(-logits, 0.0) + jnp.log1p(small))
    closed_ref[...] = jnp.where(logits >= 0, small, 1.0) / (1.0 + small)
    i = lax.broadcasted_iota(jnp.int32, (128, 128), 0)
    j = lax.broadcasted_iota(jnp.int32, (128, 128), 1)
    below = (i >= j).astype(BF)
    carry = jnp.zeros((1, 128), F32)
    for b in range(0, length, 128):
        total = exact_dot(below, log_decay[b : b + 128], NN) + carry
        decay_ref[b : b + 128, :] = total
        drow_ref[:, b : b + 128] = total.T
        carry = total[127:128]
    lane = lax.broadcasted_iota(jnp.int32, (1, 128), 1)
    i = lax.broadcasted_iota(jnp.int32, (span, span), 0)
    j = lax.broadcasted_iota(jnp.int32, (span, span), 1)
    causal = i >= j
    seg = seg_ref[...]
    for pair in range(heads // 2):
        at = pair * 128
        for begin in range(0, length, span):
            end = begin + span
            q = qkv_ref[begin:end, at : at + 128].astype(F32) * 0.125
            k = qkv_ref[:end, width + at : width + at + 128]
            v = qkv_ref[:end, 2 * width + at : 2 * width + at + 128]
            same = column_of(seg[:, begin:end]) == seg[:, :end]
            outs = []
            for side in range(2):
                h = 2 * pair + side
                own = (lane >= 64) if side else (lane < 64)
                s = dotf(jnp.where(own, q, 0.0).astype(BF), k, NT)
                s = s + decay_ref[begin:end, h : h + 1] - drow_ref[h : h + 1, :end]
                s = jnp.where(same, s, -1e30)
                last = jnp.where(causal, s[:, begin:], -1e30)
                s = jnp.concatenate([s[:, :begin], last], axis=1) if begin else last
                highest = jnp.max(s, axis=1, keepdims=True)
                p = jnp.exp(s - highest)
                total = jnp.sum(p, axis=1, keepdims=True)
                outs.append(dotf(p.astype(BF), v, NN) / total)
                stat_ref[begin:end, h : h + 1] = highest + jnp.log(total)
            mixed_ref[begin:end, at : at + 128] = jnp.where(lane < 64, *outs).astype(BF)
    rows_ref[0:8, :] = drow_ref[0:8, :]
    for b in range(0, length, 128):
        rows_ref[8:16, b : b + 128] = stat_ref[b : b + 128, :].T[0:8]
    branch_ref[...] = dotf(mixed_ref[...], w_ref[:, 3 * width + 128 :], NT).astype(BF)


def attend(x, w, bias, seg, heads):
    length, features = x.shape
    width = heads * 64
    return pl.pallas_call(
        functools.partial(attend_kernel, heads, 256),
        out_shape=(
            jax.ShapeDtypeStruct((length, 3 * width), BF),
            jax.ShapeDtypeStruct((length, width), BF),
            jax.ShapeDtypeStruct((length, features), BF),
            jax.ShapeDtypeStruct((16, length), F32),
            jax.ShapeDtypeStruct((length, 128), F32),
            jax.ShapeDtypeStruct((length, 128), F32),
        ),
        scratch_shapes=[pltpu.VMEM((length, 128), F32), pltpu.VMEM((128, length), F32)],
        compiler_params=pltpu.CompilerParams(vmem_limit_bytes=VMEM_LIMIT),
        cost_estimate=pl.CostEstimate(
            flops=12 * 10**9, bytes_accessed=2 * 10**7, transcendentals=5 * 10**6
        ),
        name="attend",
    )(x, w, bias, seg)


def attend_back_kernel(
    heads, span, m_ref, w_ref, qkv_ref, mixed_ref, rows_ref, decay_ref, closed_ref, seg_ref, grad_ref, part_ref, bias_ref, mb_ref, dq_ref, sums_ref, drow_ref
):
    length = m_ref.shape[0]
    width = heads * 64
    mb_ref[...] = dotf(m_ref[...], w_ref[:, 3 * width + 128 :], NN).astype(BF)
    lane = lax.broadcasted_iota(jnp.int32, (1, 128), 1)
    i = lax.broadcasted_iota(jnp.int32, (span, span), 0)
    j = lax.broadcasted_iota(jnp.int32, (span, span), 1)
    causal = i <= j
    seg = seg_ref[...]
    sums_ref[...] = jnp.zeros_like(sums_ref)
    drow_ref[...] = jnp.zeros_like(drow_ref)
    side_row = lax.broadcasted_iota(jnp.int32, (8, 128), 0)
    side_lane = lax.broadcasted_iota(jnp.int32, (8, 128), 1)
    chosen = ((side_lane // 64) == side_row).astype(BF)
    for pair in range(heads // 2):
        at = pair * 128
        own_product = mb_ref[:, at : at + 128].astype(F32) * mixed_ref[:, at : at + 128].astype(F32)
        delta = exact_dot(chosen, own_product, NT)
        for begin in range(0, length, span):
            end = begin + span
            k = qkv_ref[begin:end, width + at : width + at + 128]
            v = qkv_ref[begin:end, 2 * width + at : 2 * width + at + 128]
            q = qkv_ref[begin:, at : at + 128]
            mb = mb_ref[begin:, at : at + 128]
            same = column_of(seg[:, begin:end]) == seg[:, begin:]
            dks, dvs, dqs = [], [], []
            for side in range(2):
                h = 2 * pair + side
                own = (lane >= 64) if side else (lane < 64)
                own_k = jnp.where(own, k.astype(F32) * 0.125, 0.0).astype(BF)
                own_v = jnp.where(own, v.astype(F32), 0.0).astype(BF)
                s = dotf(own_k, q, NT)
                s = s + (rows_ref[h : h + 1, begin:] - rows_ref[8 + h : 9 + h, begin:])
                s = jnp.where(same, s - decay_ref[begin:end, h : h + 1], -1e30)
                first = jnp.where(causal, s[:, :span], -1e30)
                s = jnp.concatenate([first, s[:, span:]], axis=1) if end < length else first
                p = jnp.exp(s)
                dvs.append(dotf(p.astype(BF), mb, NN))
                ds = p * (dotf(own_v, mb, NT) - delta[side : side + 1, begin:])
                ds_low = (ds * 0.125).astype(BF)
                dks.append(dotf(ds_low, q, NN))
                dqs.append(dotf(ds_low, k, TN))
                sums_ref[begin:end, h : h + 1] = jnp.sum(ds, axis=1, keepdims=True)
                drow_ref[h : h + 1, begin:] += jnp.sum(ds, axis=0, keepdims=True)
            k_at, v_at = width + at, 2 * width + at
            grad_ref[begin:end, k_at : k_at + 128] = jnp.where(lane < 64, *dks).astype(BF)
            grad_ref[begin:end, v_at : v_at + 128] = jnp.where(lane < 64, *dvs).astype(BF)
            dq = jnp.where(lane < 64, *dqs)
            if begin:
                dq_ref[begin:, :] += dq
            else:
                dq_ref[...] = dq
        grad_ref[:, at : at + 128] = dq_ref[...].astype(BF)
    i = lax.broadcasted_iota(jnp.int32, (128, 128), 0)
    j = lax.broadcasted_iota(jnp.int32, (128, 128), 1)
    above = (i <= j).astype(BF)
    carry = jnp.zeros((1, 128), F32)
    bias = jnp.zeros((1, 128), F32)
    blank = jnp.zeros((120, 128), F32)
    for b in reversed(range(0, length, 128)):
        row_sum = jnp.concatenate([drow_ref[:, b : b + 128], blank], axis=0).T
        total = exact_dot(above, row_sum - sums_ref[b : b + 128, :], NN) + carry
        carry = total[0:1]
        back = (closed_ref[b : b + 128, :] * total).astype(BF)
        grad_ref[b : b + 128, 3 * width :] = back
        bias = bias + jnp.sum(back.astype(F32), axis=0, keepdims=True)
    bias_ref[...] = jnp.broadcast_to(bias, bias_ref.shape)
    part_ref[...] = dotf(grad_ref[...], w_ref[:, : 3 * width + 128], NT).astype(BF)


def attend_back(m, w, qkv, mixed, rows, decay, closed, seg, heads):
    length, features = m.shape
    width = heads * 64
    return pl.pallas_call(
        functools.partial(attend_back_kernel, heads, 256),
        out_shape=(
            jax.ShapeDtypeStruct((length, 3 * width + 128), BF),
            jax.ShapeDtypeStruct((length, features), BF),
            jax.ShapeDtypeStruct((8, 128), F32),
        ),
        scratch_shapes=[
            pltpu.VMEM((length, width), BF),
            pltpu.VMEM((length, 128), F32),
            pltpu.VMEM((length, 128), F32),
            pltpu.VMEM((8, length), F32),
        ],
        compiler_params=pltpu.CompilerParams(vmem_limit_bytes=VMEM_LIMIT),
        cost_estimate=pl.CostEstimate(
            flops=20 * 10**9, bytes_accessed=2 * 10**7, transcendentals=5 * 10**6
        ),
        name="attend_back",
    )(m, w, qkv, mixed, rows, decay, closed, seg)


def feed_kernel(x_ref, c_ref, wg_ref, wu_ref, wd_ref, hidden_ref, gb_ref, ub_ref, part_ref, total_ref):
    step = pl.program_id(0)
    x = x_ref[...]
    wg, wu = wg_ref[...], wu_ref[...]
    gate = dotf(x, wg, NN)
    up = dotf(x, wu, NN)
    back = dotf(c_ref[...], wd_ref[...], NN)
    sig = 1.0 / (1.0 + jnp.exp(-gate))
    silu = gate * sig
    hidden_ref[...] = (silu * up).astype(BF)
    gb = (back * up * sig * (1.0 + gate * (1.0 - sig))).astype(BF)
    ub = (back * silu).astype(BF)
    gb_ref[...] = gb
    ub_ref[...] = ub
    part = dotf(gb, wg, NT) + dotf(ub, wu, NT)

    @pl.when(step == 0)
    def _():
        total_ref[...] = part

    @pl.when(step > 0)
    def _():
        total_ref[...] += part

    @pl.when(step == pl.num_programs(0) - 1)
    def _():
        part_ref[...] = total_ref[...].astype(BF)


def feed(x, c, w, block=256):
    length, features = x.shape
    width = w.shape[1] // 3
    steps = width // block
    whole = pl.BlockSpec((length, features), lambda i: (0, 0))
    tall = lambda k: pl.BlockSpec((features, block), lambda i: (0, i + k * steps))
    out = pl.BlockSpec((length, block), lambda i: (0, i))
    return pl.pallas_call(
        feed_kernel,
        grid=(steps,),
        in_specs=[whole, whole, tall(0), tall(1), tall(2)],
        out_specs=[out, out, out, whole],
        out_shape=[jax.ShapeDtypeStruct((length, width), BF)] * 3
        + [jax.ShapeDtypeStruct((length, features), BF)],
        scratch_shapes=[pltpu.VMEM((length, features), F32)],
        compiler_params=pltpu.CompilerParams(vmem_limit_bytes=VMEM_LIMIT),
        cost_estimate=pl.CostEstimate(
            flops=16 * 10**9, bytes_accessed=25 * 10**6, transcendentals=10**6
        ),
        name="feed",
    )(x, c, w, w, w)


def weight_grad_kernel(steps, left, right, *refs):
    ins, out_ref = refs[:-1], refs[-1]
    step = pl.program_id(0)
    begin = 0
    for lhs, rhs, count in zip(left, right, steps):

        @pl.when((step >= begin) & (step < begin + count))
        def _():
            out_ref[...] = dotf(ins[lhs][...], ins[rhs][...], TN).astype(BF)

        begin += count


def weight_grad(lefts, rights, uses, block, name):
    length, features = lefts[0].shape
    counts = [rights[r].shape[1] // block for _, r in uses]
    starts = [sum(counts[:n]) for n in range(len(counts))]
    in_specs = [pl.BlockSpec((length, features), lambda i: (0, 0)) for _ in lefts]
    for n in range(len(rights)):
        in_specs.append(
            pl.BlockSpec(
                (length, block),
                lambda i, n=n: (0, jnp.clip(i - starts[n], 0, counts[n] - 1)),
            )
        )
    return pl.pallas_call(
        functools.partial(
            weight_grad_kernel,
            counts,
            [left for left, _ in uses],
            [len(lefts) + r for _, r in uses],
        ),
        grid=(sum(counts),),
        in_specs=in_specs,
        out_specs=pl.BlockSpec((features, block), lambda i: (0, i)),
        out_shape=jax.ShapeDtypeStruct((features, sum(counts) * block), BF),
        compiler_params=pltpu.CompilerParams(vmem_limit_bytes=VMEM_LIMIT),
        cost_estimate=pl.CostEstimate(
            flops=2 * length * features * sum(counts) * block,
            bytes_accessed=2 * features * (2 * length + sum(counts) * block),
            transcendentals=0,
        ),
        name=name,
    )(*lefts, *rights)
def attend_grads_kernel(x_ref, m_ref, grad_ref, mixed_ref, part_ref, out_ref, gain_ref):
    inner = grad_ref.shape[1]
    out_ref[:, :inner] = dotf(x_ref[...], grad_ref[...], TN).astype(BF)
    out_ref[:, inner:] = dotf(m_ref[...], mixed_ref[...], TN).astype(BF)
    total = jnp.zeros((8, gain_ref.shape[1]), F32)
    for b in range(0, x_ref.shape[0], 8):
        rows = slice(b, b + 8)
        total = total + x_ref[rows, :].astype(F32) * part_ref[rows, :].astype(F32)
    gain_ref[...] = jnp.broadcast_to(jnp.sum(total, axis=0, keepdims=True), gain_ref.shape)


def attend_grads(x, m, grads, mixed, part):
    length, features = x.shape
    columns = grads.shape[1] + mixed.shape[1]
    return pl.pallas_call(
        attend_grads_kernel,
        out_shape=(
            jax.ShapeDtypeStruct((features, columns), BF),
            jax.ShapeDtypeStruct((8, features), F32),
        ),
        compiler_params=pltpu.CompilerParams(vmem_limit_bytes=VMEM_LIMIT),
        cost_estimate=pl.CostEstimate(
            flops=2 * length * features * columns, bytes_accessed=2 * 10**7, transcendentals=0
        ),
        name="attend_grads",
    )(x, m, grads, mixed, part)


def finish_kernel(widths, odd_ref, low_ref, high_ref, a_ref, b_ref, c_ref, *out_refs):
    odd = odd_ref[0] == 1

    def put(first_ref, second_ref):
        begin = 0
        for width, out_ref in zip(widths, out_refs):
            first = first_ref[:, begin : begin + width].astype(F32)
            out_ref[...] = first + second_ref[:, begin : begin + width].astype(F32)
            begin += width

    @pl.when(odd)
    def _():
        put(c_ref, b_ref)

    @pl.when(jnp.logical_not(odd))
    def _():
        put(low_ref, a_ref)


def finish(odd, low, high, a, b, c, widths):
    rows = low.shape[0]
    return pl.pallas_call(
        functools.partial(finish_kernel, widths),
        in_specs=[pl.BlockSpec(memory_space=pltpu.SMEM)]
        + [pl.BlockSpec(memory_space=pltpu.VMEM)] * 5,
        out_shape=[jax.ShapeDtypeStruct((rows, width), F32) for width in widths],
        compiler_params=pltpu.CompilerParams(vmem_limit_bytes=VMEM_LIMIT),
        cost_estimate=pl.CostEstimate(flops=10**6, bytes_accessed=8 * 10**6, transcendentals=0),
        name="finish",
    )(odd, low, high, a, b, c)


class Layout:
    def __init__(self, dp, tensor):
        self.groups = [[core + 2 * i for i in range(dp // 2)] for core in range(2)]
        self.core = [(d, d ^ 1) for d in range(dp)]
        self.pair = [(z, z ^ 1) for z in range(tensor)]
        flat = lambda d, z: d * tensor + z
        devices = [(d, z) for d in range(dp) for z in range(tensor)]
        away = [(d, z) for d, z in devices if (d & 1) != (z >> 1)]
        near = [(d, z) for d, z in devices if (d & 1) == (z >> 1)]
        self.move = [(flat(d, z), flat(d ^ 1, z ^ 2)) for d, z in away]
        self.pair_near = [(flat(d, z), flat(d, z ^ 1)) for d, z in near]
        self.pair_away = [(flat(d, z), flat(d, z ^ 1)) for d, z in away]
        even = [(d, z) for d, z in devices if d & 1 == 0]
        odd = [(d, z) for d, z in devices if d & 1 == 1]
        self.even_far = [(flat(d, z), flat(d + 1, z ^ 2)) for d, z in even]
        self.odd_far = [(flat(d, z), flat(d, z ^ 2)) for d, z in odd]
        self.odd_even = [(flat(d, z), flat(d - 1, z)) for d, z in odd]
        self.back_even_far = [(b, a) for a, b in self.even_far]
        self.back_odd_even = [(b, a) for a, b in self.odd_even]


def cat(*parts):
    return jnp.concatenate(parts, axis=0)


def after(x, *deps):
    return lax.optimization_barrier((x, *deps))[0]


def swap_weight(lay, w, odd):
    a = lax.ppermute(w, BOTH, lay.even_far)
    b = lax.ppermute(w, BOTH, lay.odd_far)
    c = lax.ppermute(w, BOTH, lay.odd_even)
    return jnp.where(odd, cat(a, b), cat(w, c))


def gather_rows(lay, rows):
    return lax.all_gather(rows, "dp", axis=0, tiled=True, axis_index_groups=lay.groups)


def scatter_rows(lay, g):
    return lax.psum_scatter(
        g, "dp", scatter_dimension=0, tiled=True, axis_index_groups=lay.groups
    )


def share_grad(lay, r, odd, widths):
    half = r.shape[0] // 2
    low, high = r[:half], r[half:]
    a = lax.ppermute(low, BOTH, lay.back_even_far)
    b = lax.ppermute(high, BOTH, lay.odd_far)
    c = lax.ppermute(high, BOTH, lay.back_odd_even)
    return finish(odd.astype(jnp.int32).reshape(1), low, high, a, b, c, widths)


def gather_pair(lay, x):
    z = lax.ppermute(x, "tensor", lay.pair)
    near = cat(x, z)
    return cat(near, lax.ppermute(near, "dp", lay.core))


def scatter_pair_first(lay, part):
    half = part.shape[0] // 2
    got = lax.ppermute(part[half:], "dp", lay.core)
    return part[:half].astype(F32) + got.astype(F32)


def scatter_pair_second(lay, mine):
    quarter = mine.shape[0] // 2
    got = lax.ppermute(mine[quarter:].astype(BF), "tensor", lay.pair)
    return mine[:quarter] + got.astype(F32)


def gather_sequence(lay, x, odd, zodd, away):
    moved = lax.ppermute(x, BOTH, lay.move)
    near = lax.ppermute(x, BOTH, lay.pair_near)
    far = lax.ppermute(moved, BOTH, lay.pair_away)
    mine = jnp.where(away, moved, x)
    other = jnp.where(away, far, near)
    half = jnp.where(zodd, cat(other, mine), cat(mine, other))
    got = lax.ppermute(half, "dp", lay.core)
    return jnp.where(odd, cat(got, half), cat(half, got)), moved


def scatter_sequence(lay, part, odd, zodd, away):
    half = part.shape[0] // 2
    quarter = half // 2
    first, second = part[:half], part[half:]
    got = lax.ppermute(jnp.where(odd, first, second), "dp", lay.core)
    mine = jnp.where(odd, second, first).astype(F32) + got.astype(F32)
    first, second = mine[:quarter], mine[quarter:]
    got = lax.ppermute(jnp.where(zodd, first, second).astype(BF), "tensor", lay.pair)
    mine = jnp.where(zodd, second, first) + got.astype(F32)
    got = lax.ppermute(mine.astype(BF), BOTH, lay.move)
    return jnp.where(away, got.astype(F32), mine)


def sum_all(x, axis):
    size = lax.axis_size(axis)
    step = 1
    while step < size:
        x = x + lax.ppermute(x, axis, [(i, i ^ step) for i in range(size)])
        step *= 2
    return x


def inverse_rms(rows):
    return lax.rsqrt(jnp.mean(rows * rows, axis=-1, keepdims=True) + EPS)


def norm_back(rows, gain, grad):
    r = inverse_rms(rows)
    xhat = rows * r
    scaled = grad * gain
    return r * (scaled - xhat * jnp.mean(scaled * xhat, axis=-1, keepdims=True))


def per_device(
    layer_input,
    segment_ids,
    attn_gain,
    query_weight,
    key_weight,
    value_weight,
    forget_weight,
    forget_bias,
    output_weight,
    feed_gain,
    gate_weight,
    up_weight,
    down_weight,
    output_cotangent,
):
    lay = Layout(lax.axis_size("dp"), lax.axis_size("tensor"))
    z = lax.axis_index("tensor")
    odd = (lax.axis_index("dp") & 1) == 1
    zodd = (z & 1) == 1
    away = odd != (z >= 2)
    quarter = jnp.where(odd, z ^ 2, z)
    heads = forget_weight.shape[1]
    width = query_weight.shape[1]
    hidden_width = gate_weight.shape[1]
    features = layer_input.shape[1]
    forget_pad = jnp.pad(forget_weight, ((0, 0), (0, 128 - heads)))

    w_attn_local = jnp.concatenate(
        [query_weight, key_weight, value_weight, forget_pad, output_weight], axis=1
    ).astype(BF)
    attn_rows = swap_weight(lay, w_attn_local, odd)
    w_attn = gather_rows(lay, attn_rows)

    normed = (layer_input * inverse_rms(layer_input) * attn_gain).astype(BF)
    attn_normed, moved = gather_sequence(lay, after(normed, attn_rows), odd, zodd, away)
    segment = jnp.where(away, lax.ppermute(segment_ids, "dp", lay.core), segment_ids)
    seg_row = segment[None, :]
    bias = jnp.pad(
        lax.dynamic_slice_in_dim(forget_bias, quarter * heads, heads), (0, 128 - heads)
    )[None, :]

    w_feed_local = jnp.concatenate([gate_weight, up_weight, down_weight], axis=1).astype(BF)
    feed_rows = swap_weight(lay, after(w_feed_local, moved), odd)
    w_feed = gather_rows(lay, after(feed_rows, w_attn))
    cot_low = gather_pair(lay, after(output_cotangent.astype(BF), feed_rows))

    qkv, mixed, branch_part, rows, decay, closed = attend(
        attn_normed, w_attn, bias, seg_row, heads
    )
    branch = scatter_sequence(lay, after(branch_part, cot_low), odd, zodd, away)
    middle = layer_input + branch

    feed_normed = gather_pair(lay, (middle * inverse_rms(middle) * feed_gain).astype(BF))
    hidden, gate_back, up_back, feed_part = feed(feed_normed, cot_low, w_feed, 512)
    feed_sum = scatter_pair_first(lay, feed_part)
    ready = after(hidden, feed_sum)
    feed_grads = weight_grad(
        [feed_normed, cot_low],
        [gate_back, up_back, ready],
        [(0, 0), (0, 1), (1, 2)],
        512,
        "feed_grads",
    )
    feed_scattered = scatter_rows(lay, feed_grads)
    feed_normed_grad = after(scatter_pair_second(lay, feed_sum), feed_grads)

    middle_grad = output_cotangent + norm_back(middle, feed_gain, feed_normed_grad)
    middle_local = middle_grad.astype(BF)
    middle_low, _ = gather_sequence(lay, middle_local, odd, zodd, away)
    w_down = w_feed[:, 2 * hidden_width :]
    down_part = dotf(after(hidden, middle_local), w_down, NT).astype(BF)
    feed_gain_part = jnp.sum(
        after(feed_part, middle_local).astype(F32) * feed_normed.astype(F32), axis=0
    )
    feed_gain_part = feed_gain_part / feed_gain

    grads, attn_part, bias_part = attend_back(
        middle_low, w_attn, qkv, mixed, rows, decay, closed, seg_row, heads
    )
    down_sum = scatter_pair_first(lay, after(down_part, middle_low))
    layer_output = middle + scatter_pair_second(lay, down_sum)
    attn_grads, attn_gain_part = attend_grads(
        attn_normed, middle_low, after(grads, layer_output), mixed, attn_part
    )
    attn_scattered = scatter_rows(lay, after(attn_grads, feed_scattered))
    attn_gain_part = attn_gain_part[0] / attn_gain
    attn_normed_grad = scatter_sequence(lay, after(attn_part, attn_grads), odd, zodd, away)
    input_grad = middle_grad + norm_back(layer_input, attn_gain, attn_normed_grad)

    bias_full = lax.dynamic_update_slice_in_dim(
        jnp.zeros(forget_bias.shape, F32), bias_part[0, :heads], quarter * heads, 0
    )
    packed = cat(attn_gain_part, feed_gain_part, bias_full)
    size = packed.shape[0]
    packed = jnp.pad(packed, (0, -size % 1024)).reshape(-1, 128)
    packed = after(packed, input_grad)
    small = sum_all(sum_all(packed, "dp"), "tensor").reshape(-1)

    gate_shard, up_shard, down_shard = share_grad(
        lay, after(feed_scattered, small), odd, [hidden_width] * 3
    )
    query_shard, key_shard, value_shard, forget_shard, output_shard = share_grad(
        lay, after(attn_scattered, gate_shard), odd, [width, width, width, 128, width]
    )
    return (
        layer_output,
        input_grad,
        small[:features],
        query_shard,
        key_shard,
        value_shard,
        forget_shard[:, :heads],
        small[2 * features : size],
        output_shard,
        small[features : 2 * features],
        gate_shard,
        up_shard,
        down_shard,
    )


def solution(mesh):
    tokens = P(("dp", "tensor"), None)
    weight = P("dp", "tensor")
    in_specs = (
        tokens, P("dp"), P(), weight, weight, weight, weight, P(), weight, P(), weight, weight, weight, tokens,
    )
    out_specs = (
        tokens, tokens, P(), weight, weight, weight, weight, P(), weight, P(), weight, weight, weight,
    )
    return jax.shard_map(
        per_device, mesh=mesh, in_specs=in_specs, out_specs=out_specs, check_vma=False
    )
```

```python
import functools

import jax
import jax.numpy as jnp
from jax import lax
from jax.experimental import pallas as pl
from jax.experimental.pallas import tpu as pltpu
from jax.sharding import PartitionSpec as P

F32 = jnp.float32
BF = jnp.bfloat16
NT = (((1,), (1,)), ((), ()))
NN = (((1,), (0,)), ((), ()))
TN = (((0,), (0,)), ((), ()))
BOTH = ("dp", "tensor")
EPS = 1e-6


def dotf(a, b, dn):
    return lax.dot_general(a, b, dn, preferred_element_type=F32)


VMEM_LIMIT = 60 * 1024 * 1024


def split3(x):
    a = x.astype(BF)
    r = x - a.astype(F32)
    b = r.astype(BF)
    return a, b, (r - b.astype(F32)).astype(BF)


def exact_dot(left, right, dims):
    return sum(dotf(left, part, dims) for part in split3(right))


def column_of(row):
    parts = [
        jnp.broadcast_to(row[:, i : i + 128], (128, 128)).T[:, :1]
        for i in range(0, row.shape[1], 128)
    ]
    return jnp.concatenate(parts, axis=0)


def starts(place_ref, block):
    odd, zodd = place_ref[0], place_ref[1]
    return [
        pl.multiple_of(
            ((1 - odd if k >> 1 else odd) * 2 + (1 - zodd if k & 1 else zodd)) * block, block
        )
        for k in range(4)
    ]


def attend_kernel(
    heads, span, place_ref, x0_ref, x1_ref, x2_ref, x3_ref, w_ref, bias_ref, seg_ref, x_ref, qkv_ref, mixed_ref, keep_ref, send_ref, rows_ref, decay_ref, closed_ref, stat_ref, drow_ref, own_ref
):
    length = x_ref.shape[0]
    block = length // 4
    width = heads * 64
    places = starts(place_ref, block)
    for at, part_ref in zip(places, (x0_ref, x1_ref, x2_ref, x3_ref)):
        x_ref[pl.ds(at, block), :] = part_ref[...]
    x = x_ref[...]
    qkv_ref[...] = dotf(x, w_ref[:, : 3 * width], NN).astype(BF)
    logits = dotf(x, w_ref[:, 3 * width : 3 * width + 128], NN) + bias_ref[...]
    small = jnp.exp(-jnp.abs(logits))
    log_decay = -(jnp.maximum(-logits, 0.0) + jnp.log1p(small))
    closed_ref[...] = jnp.where(logits >= 0, small, 1.0) / (1.0 + small)
    i = lax.broadcasted_iota(jnp.int32, (128, 128), 0)
    j = lax.broadcasted_iota(jnp.int32, (128, 128), 1)
    below = (i >= j).astype(BF)
    carry = jnp.zeros((1, 128), F32)
    for b in range(0, length, 128):
        total = exact_dot(below, log_decay[b : b + 128], NN) + carry
        decay_ref[b : b + 128, :] = total
        drow_ref[:, b : b + 128] = total.T
        carry = total[127:128]
    lane = lax.broadcasted_iota(jnp.int32, (1, 128), 1)
    i = lax.broadcasted_iota(jnp.int32, (span, span), 0)
    j = lax.broadcasted_iota(jnp.int32, (span, span), 1)
    causal = i >= j
    seg = seg_ref[...]
    for pair in range(heads // 2):
        at = pair * 128
        for begin in range(0, length, span):
            end = begin + span
            q = qkv_ref[begin:end, at : at + 128].astype(F32) * 0.125
            k = qkv_ref[:end, width + at : width + at + 128]
            v = qkv_ref[:end, 2 * width + at : 2 * width + at + 128]
            same = column_of(seg[:, begin:end]) == seg[:, :end]
            outs = []
            for side in range(2):
                h = 2 * pair + side
                own = (lane >= 64) if side else (lane < 64)
                s = dotf(jnp.where(own, q, 0.0).astype(BF), k, NT)
                s = s + decay_ref[begin:end, h : h + 1] - drow_ref[h : h + 1, :end]
                s = jnp.where(same, s, -1e30)
                last = jnp.where(causal, s[:, begin:], -1e30)
                s = jnp.concatenate([s[:, :begin], last], axis=1) if begin else last
                highest = jnp.max(s, axis=1, keepdims=True)
                p = jnp.exp(s - highest)
                total = jnp.sum(p, axis=1, keepdims=True)
                outs.append(dotf(p.astype(BF), v, NN) / total)
                stat_ref[begin:end, h : h + 1] = highest + jnp.log(total)
            mixed_ref[begin:end, at : at + 128] = jnp.where(lane < 64, *outs).astype(BF)
    rows_ref[0:8, :] = drow_ref[0:8, :]
    for b in range(0, length, 128):
        rows_ref[8:16, b : b + 128] = stat_ref[b : b + 128, :].T[0:8]
    for n, at in enumerate(places):
        own_ref[n * block : (n + 1) * block, :] = mixed_ref[pl.ds(at, block), :]
    branch = dotf(own_ref[...], w_ref[:, 3 * width + 128 :], NT)
    keep_ref[...] = branch[: 2 * block].astype(BF)
    send_ref[...] = branch[2 * block :].astype(BF)


def in_memory(scalars, arrays):
    return [pl.BlockSpec(memory_space=pltpu.SMEM)] * scalars + [
        pl.BlockSpec(memory_space=pltpu.VMEM)
    ] * arrays


def attend(place, xs, w, bias, seg, heads):
    block, features = xs[0].shape
    length = 4 * block
    width = heads * 64
    return pl.pallas_call(
        functools.partial(attend_kernel, heads, 256),
        in_specs=in_memory(1, 7),
        out_shape=(
            jax.ShapeDtypeStruct((length, features), BF),
            jax.ShapeDtypeStruct((length, 3 * width), BF),
            jax.ShapeDtypeStruct((length, width), BF),
            jax.ShapeDtypeStruct((length // 2, features), BF),
            jax.ShapeDtypeStruct((length // 2, features), BF),
            jax.ShapeDtypeStruct((16, length), F32),
            jax.ShapeDtypeStruct((length, 128), F32),
            jax.ShapeDtypeStruct((length, 128), F32),
        ),
        scratch_shapes=[
            pltpu.VMEM((length, 128), F32),
            pltpu.VMEM((128, length), F32),
            pltpu.VMEM((length, width), BF),
        ],
        compiler_params=pltpu.CompilerParams(vmem_limit_bytes=VMEM_LIMIT),
        cost_estimate=pl.CostEstimate(
            flops=12 * 10**9, bytes_accessed=2 * 10**7, transcendentals=5 * 10**6
        ),
        name="attend",
    )(place, *xs, w, bias, seg)


def attend_back_kernel(
    heads, span, place_ref, m0_ref, m1_ref, m2_ref, m3_ref, w_ref, qkv_ref, mixed_ref, rows_ref, decay_ref, closed_ref, seg_ref, m_ref, grad_ref, keep_ref, send_ref, bias_ref, mb_ref, dq_ref, sums_ref, drow_ref, own_ref
):
    length = m_ref.shape[0]
    block = length // 4
    width = heads * 64
    places = starts(place_ref, block)
    for at, part_ref in zip(places, (m0_ref, m1_ref, m2_ref, m3_ref)):
        m_ref[pl.ds(at, block), :] = part_ref[...]
    mb_ref[...] = dotf(m_ref[...], w_ref[:, 3 * width + 128 :], NN).astype(BF)
    lane = lax.broadcasted_iota(jnp.int32, (1, 128), 1)
    i = lax.broadcasted_iota(jnp.int32, (span, span), 0)
    j = lax.broadcasted_iota(jnp.int32, (span, span), 1)
    causal = i <= j
    seg = seg_ref[...]
    sums_ref[...] = jnp.zeros_like(sums_ref)
    drow_ref[...] = jnp.zeros_like(drow_ref)
    side_row = lax.broadcasted_iota(jnp.int32, (8, 128), 0)
    side_lane = lax.broadcasted_iota(jnp.int32, (8, 128), 1)
    chosen = ((side_lane // 64) == side_row).astype(BF)
    for pair in range(heads // 2):
        at = pair * 128
        own_product = mb_ref[:, at : at + 128].astype(F32) * mixed_ref[:, at : at + 128].astype(F32)
        delta = exact_dot(chosen, own_product, NT)
        for begin in range(0, length, span):
            end = begin + span
            k = qkv_ref[begin:end, width + at : width + at + 128]
            v = qkv_ref[begin:end, 2 * width + at : 2 * width + at + 128]
            q = qkv_ref[begin:, at : at + 128]
            mb = mb_ref[begin:, at : at + 128]
            same = column_of(seg[:, begin:end]) == seg[:, begin:]
            dks, dvs, dqs = [], [], []
            for side in range(2):
                h = 2 * pair + side
                own = (lane >= 64) if side else (lane < 64)
                own_k = jnp.where(own, k.astype(F32) * 0.125, 0.0).astype(BF)
                own_v = jnp.where(own, v.astype(F32), 0.0).astype(BF)
                s = dotf(own_k, q, NT)
                s = s + (rows_ref[h : h + 1, begin:] - rows_ref[8 + h : 9 + h, begin:])
                s = jnp.where(same, s - decay_ref[begin:end, h : h + 1], -1e30)
                first = jnp.where(causal, s[:, :span], -1e30)
                s = jnp.concatenate([first, s[:, span:]], axis=1) if end < length else first
                p = jnp.exp(s)
                dvs.append(dotf(p.astype(BF), mb, NN))
                ds = p * (dotf(own_v, mb, NT) - delta[side : side + 1, begin:])
                ds_low = (ds * 0.125).astype(BF)
                dks.append(dotf(ds_low, q, NN))
                dqs.append(dotf(ds_low, k, TN))
                sums_ref[begin:end, h : h + 1] = jnp.sum(ds, axis=1, keepdims=True)
                drow_ref[h : h + 1, begin:] += jnp.sum(ds, axis=0, keepdims=True)
            k_at, v_at = width + at, 2 * width + at
            grad_ref[begin:end, k_at : k_at + 128] = jnp.where(lane < 64, *dks).astype(BF)
            grad_ref[begin:end, v_at : v_at + 128] = jnp.where(lane < 64, *dvs).astype(BF)
            dq = jnp.where(lane < 64, *dqs)
            if begin:
                dq_ref[begin:, :] += dq
            else:
                dq_ref[...] = dq
        grad_ref[:, at : at + 128] = dq_ref[...].astype(BF)
    i = lax.broadcasted_iota(jnp.int32, (128, 128), 0)
    j = lax.broadcasted_iota(jnp.int32, (128, 128), 1)
    above = (i <= j).astype(BF)
    carry = jnp.zeros((1, 128), F32)
    bias = jnp.zeros((1, 128), F32)
    blank = jnp.zeros((120, 128), F32)
    for b in reversed(range(0, length, 128)):
        row_sum = jnp.concatenate([drow_ref[:, b : b + 128], blank], axis=0).T
        total = exact_dot(above, row_sum - sums_ref[b : b + 128, :], NN) + carry
        carry = total[0:1]
        back = (closed_ref[b : b + 128, :] * total).astype(BF)
        grad_ref[b : b + 128, 3 * width :] = back
        bias = bias + jnp.sum(back.astype(F32), axis=0, keepdims=True)
    bias_ref[...] = jnp.broadcast_to(bias, bias_ref.shape)
    for n, at in enumerate(places):
        own_ref[n * block : (n + 1) * block, :] = grad_ref[pl.ds(at, block), :]
    part = dotf(own_ref[...], w_ref[:, : 3 * width + 128], NT)
    keep_ref[...] = part[: 2 * block].astype(BF)
    send_ref[...] = part[2 * block :].astype(BF)


def attend_back(place, ms, w, qkv, mixed, rows, decay, closed, seg, heads):
    block, features = ms[0].shape
    length = 4 * block
    width = heads * 64
    return pl.pallas_call(
        functools.partial(attend_back_kernel, heads, 256),
        in_specs=in_memory(1, 11),
        out_shape=(
            jax.ShapeDtypeStruct((length, features), BF),
            jax.ShapeDtypeStruct((length, 3 * width + 128), BF),
            jax.ShapeDtypeStruct((length // 2, features), BF),
            jax.ShapeDtypeStruct((length // 2, features), BF),
            jax.ShapeDtypeStruct((8, 128), F32),
        ),
        scratch_shapes=[
            pltpu.VMEM((length, width), BF),
            pltpu.VMEM((length, 128), F32),
            pltpu.VMEM((length, 128), F32),
            pltpu.VMEM((8, length), F32),
            pltpu.VMEM((length, 3 * width + 128), BF),
        ],
        compiler_params=pltpu.CompilerParams(vmem_limit_bytes=VMEM_LIMIT),
        cost_estimate=pl.CostEstimate(
            flops=150 * 10**9, bytes_accessed=2 * 10**7, transcendentals=5 * 10**6
        ),
        name="attend_back",
    )(place, *ms, w, qkv, mixed, rows, decay, closed, seg)


def feed_kernel(*refs):
    x_parts, c_parts = refs[:4], refs[4:8]
    wg_ref, wu_ref, wd_ref, hidden_ref, gb_ref, ub_ref, x_ref, c_ref, keep_ref, send_ref, total_ref = refs[8:]
    step = pl.program_id(0)
    block = x_ref.shape[0] // 4

    @pl.when(step == 0)
    def _():
        for n in range(4):
            x_ref[n * block : (n + 1) * block, :] = x_parts[n][...]
            c_ref[n * block : (n + 1) * block, :] = c_parts[n][...]

    x = x_ref[...]
    wg, wu = wg_ref[...], wu_ref[...]
    gate = dotf(x, wg, NN)
    up = dotf(x, wu, NN)
    back = dotf(c_ref[...], wd_ref[...], NN)
    sig = 1.0 / (1.0 + jnp.exp(-gate))
    silu = gate * sig
    hidden_ref[...] = (silu * up).astype(BF)
    gb = (back * up * sig * (1.0 + gate * (1.0 - sig))).astype(BF)
    ub = (back * silu).astype(BF)
    gb_ref[...] = gb
    ub_ref[...] = ub
    part = dotf(gb, wg, NT) + dotf(ub, wu, NT)

    @pl.when(step == 0)
    def _():
        total_ref[...] = part

    @pl.when(step > 0)
    def _():
        total_ref[...] += part

    @pl.when(step == pl.num_programs(0) - 1)
    def _():
        keep_ref[...] = total_ref[: 2 * block].astype(BF)
        send_ref[...] = total_ref[2 * block :].astype(BF)


def feed(xs, cs, w, block=256):
    rows, features = xs[0].shape
    length = 4 * rows
    width = w.shape[1] // 3
    steps = width // block
    part = pl.BlockSpec((rows, features), lambda i: (0, 0))
    half = pl.BlockSpec((2 * rows, features), lambda i: (0, 0))
    whole = pl.BlockSpec((length, features), lambda i: (0, 0))
    tall = lambda k: pl.BlockSpec((features, block), lambda i: (0, i + k * steps))
    out = pl.BlockSpec((length, block), lambda i: (0, i))
    return pl.pallas_call(
        feed_kernel,
        grid=(steps,),
        in_specs=[part] * 8 + [tall(0), tall(1), tall(2)],
        out_specs=[out, out, out, whole, whole, half, half],
        out_shape=[jax.ShapeDtypeStruct((length, width), BF)] * 3
        + [jax.ShapeDtypeStruct((length, features), BF)] * 2
        + [jax.ShapeDtypeStruct((2 * rows, features), BF)] * 2,
        scratch_shapes=[pltpu.VMEM((length, features), F32)],
        compiler_params=pltpu.CompilerParams(vmem_limit_bytes=VMEM_LIMIT),
        cost_estimate=pl.CostEstimate(
            flops=16 * 10**9, bytes_accessed=25 * 10**6, transcendentals=10**6
        ),
        name="feed",
    )(*xs, *cs, w, w, w)


def weight_grad_kernel(steps, left, right, *refs):
    ins, out_ref = refs[:-1], refs[-1]
    step = pl.program_id(0)
    begin = 0
    for lhs, rhs, count in zip(left, right, steps):

        @pl.when((step >= begin) & (step < begin + count))
        def _():
            out_ref[...] = dotf(ins[lhs][...], ins[rhs][...], TN).astype(BF)

        begin += count


def weight_grad(lefts, rights, uses, block, name):
    length, features = lefts[0].shape
    counts = [rights[r].shape[1] // block for _, r in uses]
    starts = [sum(counts[:n]) for n in range(len(counts))]
    in_specs = [pl.BlockSpec((length, features), lambda i: (0, 0)) for _ in lefts]
    for n in range(len(rights)):
        in_specs.append(
            pl.BlockSpec(
                (length, block),
                lambda i, n=n: (0, jnp.clip(i - starts[n], 0, counts[n] - 1)),
            )
        )
    return pl.pallas_call(
        functools.partial(
            weight_grad_kernel,
            counts,
            [left for left, _ in uses],
            [len(lefts) + r for _, r in uses],
        ),
        grid=(sum(counts),),
        in_specs=in_specs,
        out_specs=pl.BlockSpec((features, block), lambda i: (0, i)),
        out_shape=jax.ShapeDtypeStruct((features, sum(counts) * block), BF),
        compiler_params=pltpu.CompilerParams(vmem_limit_bytes=VMEM_LIMIT),
        cost_estimate=pl.CostEstimate(
            flops=2 * length * features * sum(counts) * block,
            bytes_accessed=2 * features * (2 * length + sum(counts) * block),
            transcendentals=0,
        ),
        name=name,
    )(*lefts, *rights)
def attend_grads_kernel(
    place_ref, x_ref, m_ref, grad_ref, mixed_ref, keep_ref, send_ref, out_ref, gain_ref
):
    inner = grad_ref.shape[1]
    out_ref[:, :inner] = dotf(x_ref[...], grad_ref[...], TN).astype(BF)
    out_ref[:, inner:] = dotf(m_ref[...], mixed_ref[...], TN).astype(BF)
    block = x_ref.shape[0] // 4
    total = jnp.zeros((1, gain_ref.shape[1]), F32)
    for n, at in enumerate(starts(place_ref, block)):
        part = (send_ref if n >> 1 else keep_ref)[(n & 1) * block : ((n & 1) + 1) * block, :]
        own = x_ref[pl.ds(at, block), :].astype(F32) * part.astype(F32)
        total = total + jnp.sum(own, axis=0, keepdims=True)
    gain_ref[...] = jnp.broadcast_to(total, gain_ref.shape)


def attend_grads(place, x, m, grads, mixed, keep, send):
    length, features = x.shape
    columns = grads.shape[1] + mixed.shape[1]
    return pl.pallas_call(
        attend_grads_kernel,
        in_specs=in_memory(1, 6),
        out_shape=(
            jax.ShapeDtypeStruct((features, columns), BF),
            jax.ShapeDtypeStruct((8, features), F32),
        ),
        compiler_params=pltpu.CompilerParams(vmem_limit_bytes=VMEM_LIMIT),
        cost_estimate=pl.CostEstimate(
            flops=2 * length * features * columns, bytes_accessed=2 * 10**7, transcendentals=0
        ),
        name="attend_grads",
    )(place, x, m, grads, mixed, keep, send)


def finish_kernel(widths, odd_ref, low_ref, high_ref, a_ref, b_ref, c_ref, *out_refs):
    odd = odd_ref[0] == 1

    def put(first_ref, second_ref):
        begin = 0
        for width, out_ref in zip(widths, out_refs):
            first = first_ref[:, begin : begin + width].astype(F32)
            out_ref[...] = first + second_ref[:, begin : begin + width].astype(F32)
            begin += width

    @pl.when(odd)
    def _():
        put(c_ref, b_ref)

    @pl.when(jnp.logical_not(odd))
    def _():
        put(low_ref, a_ref)


def finish(odd, low, high, a, b, c, widths):
    rows = low.shape[0]
    return pl.pallas_call(
        functools.partial(finish_kernel, widths),
        in_specs=in_memory(1, 5),
        out_shape=[jax.ShapeDtypeStruct((rows, width), F32) for width in widths],
        compiler_params=pltpu.CompilerParams(vmem_limit_bytes=VMEM_LIMIT),
        cost_estimate=pl.CostEstimate(flops=10**6, bytes_accessed=8 * 10**6, transcendentals=0),
        name="finish",
    )(odd, low, high, a, b, c)


class Layout:
    def __init__(self, dp, tensor):
        self.groups = [[core + 2 * i for i in range(dp // 2)] for core in range(2)]
        self.core = [(d, d ^ 1) for d in range(dp)]
        self.pair = [(z, z ^ 1) for z in range(tensor)]
        flat = lambda d, z: d * tensor + z
        devices = [(d, z) for d in range(dp) for z in range(tensor)]
        away = [(d, z) for d, z in devices if (d & 1) != (z >> 1)]
        self.move = [(flat(d, z), flat(d ^ 1, z ^ 2)) for d, z in away]
        even = [(d, z) for d, z in devices if d & 1 == 0]
        odd = [(d, z) for d, z in devices if d & 1 == 1]
        self.even_far = [(flat(d, z), flat(d + 1, z ^ 2)) for d, z in even]
        self.odd_far = [(flat(d, z), flat(d, z ^ 2)) for d, z in odd]
        self.odd_even = [(flat(d, z), flat(d - 1, z)) for d, z in odd]
        self.back_even_far = [(b, a) for a, b in self.even_far]
        self.back_odd_even = [(b, a) for a, b in self.odd_even]


def cat(*parts):
    return jnp.concatenate(parts, axis=0)


def after(x, *deps):
    return lax.optimization_barrier((x, *deps))[0]


def swap_weight(lay, w, odd, *deps):
    a = lax.ppermute(w, BOTH, lay.even_far)
    b = lax.ppermute(w, BOTH, lay.odd_far)
    c = lax.ppermute(w, BOTH, lay.odd_even)
    return jnp.where(odd, cat(after(a, *deps), b), cat(w, c))


def gather_rows(lay, rows):
    return lax.all_gather(rows, "dp", axis=0, tiled=True, axis_index_groups=lay.groups)


def scatter_rows(lay, g):
    return lax.psum_scatter(
        g, "dp", scatter_dimension=0, tiled=True, axis_index_groups=lay.groups
    )


def share_grad(lay, r, odd, widths):
    half = r.shape[0] // 2
    low, high = r[:half], r[half:]
    a = lax.ppermute(low, BOTH, lay.back_even_far)
    b = lax.ppermute(high, BOTH, lay.odd_far)
    c = lax.ppermute(high, BOTH, lay.back_odd_even)
    return finish(odd.astype(jnp.int32).reshape(1), low, high, a, b, c, widths)


def gather_pair(lay, x, *deps):
    core = lax.ppermute(x, "dp", lay.core)
    z = lax.ppermute(x, "tensor", lay.pair)
    return x, z, core, lax.ppermute(after(z, *deps), "dp", lay.core)


def scatter_core(lay, keep, send):
    got = lax.ppermute(send, "dp", lay.core)
    half = keep.shape[0] // 2
    mine = keep[:half].astype(F32) + got[:half].astype(F32)
    other = keep[half:].astype(F32) + got[half:].astype(F32)
    return mine, other.astype(BF)


def scatter_z(lay, mine, other):
    return mine + lax.ppermute(other, "tensor", lay.pair).astype(F32)


def sum_all(x, axis):
    size = lax.axis_size(axis)
    step = 1
    while step < size:
        x = x + lax.ppermute(x, axis, [(i, i ^ step) for i in range(size)])
        step *= 2
    return x


def inverse_rms(rows):
    return lax.rsqrt(jnp.mean(rows * rows, axis=-1, keepdims=True) + EPS)


def norm_back(rows, gain, grad):
    r = inverse_rms(rows)
    xhat = rows * r
    scaled = grad * gain
    return r * (scaled - xhat * jnp.mean(scaled * xhat, axis=-1, keepdims=True))


def per_device(
    layer_input,
    segment_ids,
    attn_gain,
    query_weight,
    key_weight,
    value_weight,
    forget_weight,
    forget_bias,
    output_weight,
    feed_gain,
    gate_weight,
    up_weight,
    down_weight,
    output_cotangent,
):
    lay = Layout(lax.axis_size("dp"), lax.axis_size("tensor"))
    z = lax.axis_index("tensor")
    odd = (lax.axis_index("dp") & 1) == 1
    zodd = (z & 1) == 1
    away = odd != (z >= 2)
    quarter = jnp.where(odd, z ^ 2, z)
    heads = forget_weight.shape[1]
    width = query_weight.shape[1]
    hidden_width = gate_weight.shape[1]
    features = layer_input.shape[1]
    place = jnp.stack([odd, zodd]).astype(jnp.int32)

    def moved(x):
        return jnp.where(away, lax.ppermute(x, BOTH, lay.move), x)

    def moved_back(x):
        low = lax.ppermute(x.astype(BF), BOTH, lay.move)
        return jnp.where(away, low.astype(F32), x)

    forget_pad = jnp.pad(forget_weight, ((0, 0), (0, 128 - heads)))
    w_attn_local = jnp.concatenate(
        [query_weight, key_weight, value_weight, forget_pad, output_weight], axis=1
    ).astype(BF)
    attn_rows = swap_weight(lay, w_attn_local, odd)
    w_attn = gather_rows(lay, attn_rows)
    w_feed_local = jnp.concatenate([gate_weight, up_weight, down_weight], axis=1).astype(BF)
    feed_rows = swap_weight(lay, after(w_feed_local, attn_rows), odd)
    w_feed = gather_rows(lay, feed_rows)
    segment = jnp.where(
        away, lax.ppermute(after(segment_ids, attn_rows), "dp", lay.core), segment_ids
    )
    seg_row = segment[None, :]
    bias = jnp.pad(
        lax.dynamic_slice_in_dim(forget_bias, quarter * heads, heads), (0, 128 - heads)
    )[None, :]

    layer = moved_back(after(layer_input, feed_rows))
    normed = (layer * inverse_rms(layer) * attn_gain).astype(BF)
    xs = gather_pair(lay, normed)
    cot_low = moved(after(output_cotangent.astype(BF), normed))
    cot_z = lax.ppermute(after(cot_low, xs[1]), "tensor", lay.pair)
    attn_normed, qkv, mixed, keep, send, rows, decay, closed = attend(
        place, (*xs[:3], after(xs[3], cot_low)), w_attn, bias, seg_row, heads
    )
    mine, other = scatter_core(lay, keep, after(send, cot_z))
    cots = (
        cot_low,
        cot_z,
        lax.ppermute(after(cot_low, other), "dp", lay.core),
        lax.ppermute(after(cot_z, other), "dp", lay.core),
    )
    branch = scatter_z(lay, mine, other)
    middle = layer + branch

    feeds = gather_pair(lay, (middle * inverse_rms(middle) * feed_gain).astype(BF))
    hidden, gate_back, up_back, feed_normed, cot_all, keep, send = feed(feeds, cots, w_feed, 512)
    feed_keep, feed_send = keep, send
    mine, other = scatter_core(lay, keep, send)
    hidden, other = lax.optimization_barrier((hidden, other))
    got = lax.ppermute(other, "tensor", lay.pair)
    feed_grads = weight_grad(
        [feed_normed, cot_all],
        [gate_back, up_back, hidden],
        [(0, 0), (0, 1), (1, 2)],
        512,
        "feed_grads",
    )
    feed_scattered = scatter_rows(lay, feed_grads)
    feed_normed_grad = after(mine + got.astype(F32), feed_grads)

    middle_part = norm_back(middle, feed_gain, feed_normed_grad)
    cotangent = jnp.where(away, cot_low.astype(F32), output_cotangent)
    middle_low = (cotangent + middle_part).astype(BF)
    ms = gather_pair(lay, middle_low)
    w_down = w_feed[:, 2 * hidden_width :]
    ready = after(hidden, middle_low)
    half = hidden.shape[0] // 2
    down_send = dotf(ready[half:], w_down, NT).astype(BF)
    down_keep = dotf(ready[:half], w_down, NT).astype(BF)
    near, far = feed_normed[:half].astype(F32), feed_normed[half:].astype(F32)
    feed_gain_part = jnp.sum(
        after(feed_keep, middle_low).astype(F32) * near + feed_send.astype(F32) * far, axis=0
    )
    feed_gain_part = feed_gain_part / feed_gain
    mine, other = scatter_core(lay, down_keep, down_send)
    ms = (*ms[:3], after(ms[3], other))

    middle_all, grads, keep, send, bias_part = attend_back(
        place, ms, w_attn, qkv, mixed, rows, decay, closed, seg_row, heads
    )
    down = branch + scatter_z(lay, mine, other)
    down_back = moved_back(down)
    attn_grads, attn_gain_part = attend_grads(
        place, attn_normed, middle_all, after(grads, down), mixed, keep, send
    )
    layer_output = layer_input + down_back
    bias_full = lax.dynamic_update_slice_in_dim(
        jnp.zeros(forget_bias.shape, F32), bias_part[0, :heads], quarter * heads, 0
    )
    packed = cat(attn_gain_part[0] / attn_gain, feed_gain_part, bias_full)
    size = packed.shape[0]
    packed = jnp.pad(packed, (0, -size % 1024)).reshape(-1, 128)
    packed = sum_all(after(packed, down_back), "tensor")
    attn_scattered = scatter_rows(lay, after(attn_grads, feed_scattered, packed))
    gate_shard, up_shard, down_shard = share_grad(
        lay, after(feed_scattered, packed), odd, [hidden_width] * 3
    )
    mine, other = scatter_core(lay, keep, after(send, packed))
    attn_normed_grad = scatter_z(lay, mine, other)
    input_part = norm_back(layer, attn_gain, attn_normed_grad)
    input_back = moved_back(after(middle_part + input_part, gate_shard))
    input_grad = output_cotangent + input_back
    small = sum_all(after(packed, other), "dp").reshape(-1)

    query_shard, key_shard, value_shard, forget_shard, output_shard = share_grad(
        lay,
        after(attn_scattered, small, gate_shard, input_back),
        odd,
        [width, width, width, 128, width],
    )
    return (
        layer_output,
        input_grad,
        small[:features],
        query_shard,
        key_shard,
        value_shard,
        forget_shard[:, :heads],
        small[2 * features : size],
        output_shard,
        small[features : 2 * features],
        gate_shard,
        up_shard,
        down_shard,
    )


def solution(mesh):
    tokens = P(("dp", "tensor"), None)
    weight = P("dp", "tensor")
    in_specs = (
        tokens, P("dp"), P(), weight, weight, weight, weight, P(), weight, P(), weight, weight, weight, tokens,
    )
    out_specs = (
        tokens, tokens, P(), weight, weight, weight, weight, P(), weight, P(), weight, weight, weight,
    )
    return jax.shard_map(
        per_device, mesh=mesh, in_specs=in_specs, out_specs=out_specs, check_vma=False
    )
```

```python
import functools

import jax
import jax.numpy as jnp
from jax import lax
from jax.experimental import pallas as pl
from jax.experimental.pallas import tpu as pltpu
from jax.sharding import PartitionSpec as P

F32 = jnp.float32
BF = jnp.bfloat16
NT = (((1,), (1,)), ((), ()))
NN = (((1,), (0,)), ((), ()))
TN = (((0,), (0,)), ((), ()))
BOTH = ("dp", "tensor")
EPS = 1e-6


def dotf(a, b, dn):
    return lax.dot_general(a, b, dn, preferred_element_type=F32)


VMEM_LIMIT = 38 * 1024 * 1024


def split3(x):
    a = x.astype(BF)
    r = x - a.astype(F32)
    b = r.astype(BF)
    return a, b, (r - b.astype(F32)).astype(BF)


def exact_dot(left, right, dims):
    return sum(dotf(left, part, dims) for part in split3(right))


def column_of(row):
    parts = [
        jnp.broadcast_to(row[:, i : i + 128], (128, 128)).T[:, :1]
        for i in range(0, row.shape[1], 128)
    ]
    return jnp.concatenate(parts, axis=0)


def starts(place_ref, block):
    odd, zodd = place_ref[0], place_ref[1]
    return [
        pl.multiple_of(
            ((1 - odd if k >> 1 else odd) * 2 + (1 - zodd if k & 1 else zodd)) * block, block
        )
        for k in range(4)
    ]


def attend_kernel(
    heads, span, place_ref, x0_ref, x1_ref, x2_ref, x3_ref, w_ref, bias_ref, seg_ref, x_ref, qkv_ref, mixed_ref, keep_ref, send_ref, rows_ref, decay_ref, closed_ref, stat_ref, drow_ref, own_ref
):
    length = x_ref.shape[0]
    block = length // 4
    width = heads * 64
    places = starts(place_ref, block)
    for at, part_ref in zip(places, (x0_ref, x1_ref, x2_ref, x3_ref)):
        x_ref[pl.ds(at, block), :] = part_ref[...]
    x = x_ref[...]
    qkv_ref[...] = dotf(x, w_ref[:, : 3 * width], NN).astype(BF)
    logits = dotf(x, w_ref[:, 3 * width : 3 * width + 128], NN) + bias_ref[...]
    small = jnp.exp(-jnp.abs(logits))
    log_decay = -(jnp.maximum(-logits, 0.0) + jnp.log1p(small))
    closed_ref[...] = jnp.where(logits >= 0, small, 1.0) / (1.0 + small)
    i = lax.broadcasted_iota(jnp.int32, (128, 128), 0)
    j = lax.broadcasted_iota(jnp.int32, (128, 128), 1)
    below = (i >= j).astype(BF)
    carry = jnp.zeros((1, 128), F32)
    for b in range(0, length, 128):
        total = exact_dot(below, log_decay[b : b + 128], NN) + carry
        decay_ref[b : b + 128, :] = total
        drow_ref[:, b : b + 128] = total.T
        carry = total[127:128]
    lane = lax.broadcasted_iota(jnp.int32, (1, 128), 1)
    i = lax.broadcasted_iota(jnp.int32, (span, span), 0)
    j = lax.broadcasted_iota(jnp.int32, (span, span), 1)
    causal = i >= j
    seg = seg_ref[...]
    for pair in range(heads // 2):
        at = pair * 128
        for begin in range(0, length, span):
            end = begin + span
            q = qkv_ref[begin:end, at : at + 128].astype(F32) * 0.125
            k = qkv_ref[:end, width + at : width + at + 128]
            v = qkv_ref[:end, 2 * width + at : 2 * width + at + 128]
            same = column_of(seg[:, begin:end]) == seg[:, :end]
            outs = []
            for side in range(2):
                h = 2 * pair + side
                own = (lane >= 64) if side else (lane < 64)
                s = dotf(jnp.where(own, q, 0.0).astype(BF), k, NT)
                s = s + decay_ref[begin:end, h : h + 1] - drow_ref[h : h + 1, :end]
                s = jnp.where(same, s, -1e30)
                last = jnp.where(causal, s[:, begin:], -1e30)
                s = jnp.concatenate([s[:, :begin], last], axis=1) if begin else last
                highest = jnp.max(s, axis=1, keepdims=True)
                p = jnp.exp(s - highest)
                total = jnp.sum(p, axis=1, keepdims=True)
                outs.append(dotf(p.astype(BF), v, NN) / total)
                stat_ref[begin:end, h : h + 1] = highest + jnp.log(total)
            mixed_ref[begin:end, at : at + 128] = jnp.where(lane < 64, *outs).astype(BF)
    rows_ref[0:8, :] = drow_ref[0:8, :]
    for b in range(0, length, 128):
        rows_ref[8:16, b : b + 128] = stat_ref[b : b + 128, :].T[0:8]
    for n, at in enumerate(places):
        own_ref[n * block : (n + 1) * block, :] = mixed_ref[pl.ds(at, block), :]
    branch = dotf(own_ref[...], w_ref[:, 3 * width + 128 :], NT)
    keep_ref[...] = branch[: 2 * block].astype(BF)
    send_ref[...] = branch[2 * block :].astype(BF)


def in_memory(scalars, arrays):
    return [pl.BlockSpec(memory_space=pltpu.SMEM)] * scalars + [
        pl.BlockSpec(memory_space=pltpu.VMEM)
    ] * arrays


def attend(place, xs, w, bias, seg, heads):
    block, features = xs[0].shape
    length = 4 * block
    width = heads * 64
    return pl.pallas_call(
        functools.partial(attend_kernel, heads, 256),
        in_specs=in_memory(1, 7),
        out_shape=(
            jax.ShapeDtypeStruct((length, features), BF),
            jax.ShapeDtypeStruct((length, 3 * width), BF),
            jax.ShapeDtypeStruct((length, width), BF),
            jax.ShapeDtypeStruct((length // 2, features), BF),
            jax.ShapeDtypeStruct((length // 2, features), BF),
            jax.ShapeDtypeStruct((16, length), F32),
            jax.ShapeDtypeStruct((length, 128), F32),
            jax.ShapeDtypeStruct((length, 128), F32),
        ),
        scratch_shapes=[
            pltpu.VMEM((length, 128), F32),
            pltpu.VMEM((128, length), F32),
            pltpu.VMEM((length, width), BF),
        ],
        compiler_params=pltpu.CompilerParams(vmem_limit_bytes=VMEM_LIMIT),
        cost_estimate=pl.CostEstimate(
            flops=12 * 10**9, bytes_accessed=2 * 10**7, transcendentals=5 * 10**6
        ),
        name="attend",
    )(place, *xs, w, bias, seg)


def attend_back_kernel(
    heads, span, place_ref, m0_ref, m1_ref, m2_ref, m3_ref, w_ref, qkv_ref, mixed_ref, rows_ref, decay_ref, closed_ref, seg_ref, m_ref, grad_ref, keep_ref, send_ref, bias_ref, mb_ref, dq_ref, sums_ref, drow_ref, own_ref
):
    length = m_ref.shape[0]
    block = length // 4
    width = heads * 64
    places = starts(place_ref, block)
    for at, part_ref in zip(places, (m0_ref, m1_ref, m2_ref, m3_ref)):
        m_ref[pl.ds(at, block), :] = part_ref[...]
    mb_ref[...] = dotf(m_ref[...], w_ref[:, 3 * width + 128 :], NN).astype(BF)
    lane = lax.broadcasted_iota(jnp.int32, (1, 128), 1)
    i = lax.broadcasted_iota(jnp.int32, (span, span), 0)
    j = lax.broadcasted_iota(jnp.int32, (span, span), 1)
    causal = i <= j
    seg = seg_ref[...]
    sums_ref[...] = jnp.zeros_like(sums_ref)
    drow_ref[...] = jnp.zeros_like(drow_ref)
    side_row = lax.broadcasted_iota(jnp.int32, (8, 128), 0)
    side_lane = lax.broadcasted_iota(jnp.int32, (8, 128), 1)
    chosen = ((side_lane // 64) == side_row).astype(BF)
    for pair in range(heads // 2):
        at = pair * 128
        own_product = mb_ref[:, at : at + 128].astype(F32) * mixed_ref[:, at : at + 128].astype(F32)
        delta = exact_dot(chosen, own_product, NT)
        for begin in range(0, length, span):
            end = begin + span
            k = qkv_ref[begin:end, width + at : width + at + 128]
            v = qkv_ref[begin:end, 2 * width + at : 2 * width + at + 128]
            q = qkv_ref[begin:, at : at + 128]
            mb = mb_ref[begin:, at : at + 128]
            same = column_of(seg[:, begin:end]) == seg[:, begin:]
            dks, dvs, dqs = [], [], []
            for side in range(2):
                h = 2 * pair + side
                own = (lane >= 64) if side else (lane < 64)
                own_k = jnp.where(own, k.astype(F32) * 0.125, 0.0).astype(BF)
                own_v = jnp.where(own, v.astype(F32), 0.0).astype(BF)
                s = dotf(own_k, q, NT)
                s = s + (rows_ref[h : h + 1, begin:] - rows_ref[8 + h : 9 + h, begin:])
                s = jnp.where(same, s - decay_ref[begin:end, h : h + 1], -1e30)
                first = jnp.where(causal, s[:, :span], -1e30)
                s = jnp.concatenate([first, s[:, span:]], axis=1) if end < length else first
                p = jnp.exp(s)
                dvs.append(dotf(p.astype(BF), mb, NN))
                ds = p * (dotf(own_v, mb, NT) - delta[side : side + 1, begin:])
                ds_low = (ds * 0.125).astype(BF)
                dks.append(dotf(ds_low, q, NN))
                dqs.append(dotf(ds_low, k, TN))
                sums_ref[begin:end, h : h + 1] = jnp.sum(ds, axis=1, keepdims=True)
                drow_ref[h : h + 1, begin:] += jnp.sum(ds, axis=0, keepdims=True)
            k_at, v_at = width + at, 2 * width + at
            grad_ref[begin:end, k_at : k_at + 128] = jnp.where(lane < 64, *dks).astype(BF)
            grad_ref[begin:end, v_at : v_at + 128] = jnp.where(lane < 64, *dvs).astype(BF)
            dq = jnp.where(lane < 64, *dqs)
            if begin:
                dq_ref[begin:, :] += dq
            else:
                dq_ref[...] = dq
        grad_ref[:, at : at + 128] = dq_ref[...].astype(BF)
    i = lax.broadcasted_iota(jnp.int32, (128, 128), 0)
    j = lax.broadcasted_iota(jnp.int32, (128, 128), 1)
    above = (i <= j).astype(BF)
    carry = jnp.zeros((1, 128), F32)
    bias = jnp.zeros((1, 128), F32)
    blank = jnp.zeros((120, 128), F32)
    for b in reversed(range(0, length, 128)):
        row_sum = jnp.concatenate([drow_ref[:, b : b + 128], blank], axis=0).T
        total = exact_dot(above, row_sum - sums_ref[b : b + 128, :], NN) + carry
        carry = total[0:1]
        back = (closed_ref[b : b + 128, :] * total).astype(BF)
        grad_ref[b : b + 128, 3 * width :] = back
        bias = bias + jnp.sum(back.astype(F32), axis=0, keepdims=True)
    bias_ref[...] = jnp.broadcast_to(bias, bias_ref.shape)
    for n, at in enumerate(places):
        own_ref[n * block : (n + 1) * block, :] = grad_ref[pl.ds(at, block), :]
    part = dotf(own_ref[...], w_ref[:, : 3 * width + 128], NT)
    keep_ref[...] = part[: 2 * block].astype(BF)
    send_ref[...] = part[2 * block :].astype(BF)


def attend_back(place, ms, w, qkv, mixed, rows, decay, closed, seg, heads):
    block, features = ms[0].shape
    length = 4 * block
    width = heads * 64
    return pl.pallas_call(
        functools.partial(attend_back_kernel, heads, 256),
        in_specs=in_memory(1, 11),
        out_shape=(
            jax.ShapeDtypeStruct((length, features), BF),
            jax.ShapeDtypeStruct((length, 3 * width + 128), BF),
            jax.ShapeDtypeStruct((length // 2, features), BF),
            jax.ShapeDtypeStruct((length // 2, features), BF),
            jax.ShapeDtypeStruct((8, 128), F32),
        ),
        scratch_shapes=[
            pltpu.VMEM((length, width), BF),
            pltpu.VMEM((length, 128), F32),
            pltpu.VMEM((length, 128), F32),
            pltpu.VMEM((8, length), F32),
            pltpu.VMEM((length, 3 * width + 128), BF),
        ],
        compiler_params=pltpu.CompilerParams(vmem_limit_bytes=VMEM_LIMIT),
        cost_estimate=pl.CostEstimate(
            flops=150 * 10**9, bytes_accessed=2 * 10**7, transcendentals=5 * 10**6
        ),
        name="attend_back",
    )(place, *ms, w, qkv, mixed, rows, decay, closed, seg)


def feed_kernel(*refs):
    x_parts, c_parts = refs[:2], refs[2:4]
    wg_ref, wu_ref, wd_ref, hidden_ref, back_ref, x_ref, c_ref, keep_ref, send_ref, total_ref = refs[4:]
    step = pl.program_id(0)
    block = x_ref.shape[0] // 2
    columns = wg_ref.shape[1]

    @pl.when(step == 0)
    def _():
        for n in range(2):
            x_ref[n * block : (n + 1) * block, :] = x_parts[n][...]
            c_ref[n * block : (n + 1) * block, :] = c_parts[n][...]

    x = x_ref[...]
    wg, wu = wg_ref[...], wu_ref[...]
    gate = dotf(x, wg, NN)
    up = dotf(x, wu, NN)
    back = dotf(c_ref[...], wd_ref[...], NN)
    sig = 1.0 / (1.0 + jnp.exp(-gate))
    silu = gate * sig
    hidden_ref[...] = (silu * up).astype(BF)
    back_ref[:, :columns] = (back * up * sig * (1.0 + gate * (1.0 - sig))).astype(BF)
    back_ref[:, columns:] = (back * silu).astype(BF)
    part = dotf(back_ref[...], jnp.concatenate([wg, wu], axis=1), NT)

    @pl.when(step == 0)
    def _():
        total_ref[...] = part

    @pl.when((step > 0) & (step < pl.num_programs(0) - 1))
    def _():
        total_ref[...] += part

    @pl.when(step == pl.num_programs(0) - 1)
    def _():
        keep_ref[...] = (total_ref[:block] + part[:block]).astype(BF)
        send_ref[...] = (total_ref[block:] + part[block:]).astype(BF)


def feed(xs, cs, w, columns):
    rows, features = xs[0].shape
    length = 2 * rows
    width = w.shape[1] // 3
    steps = width // columns
    part = pl.BlockSpec((rows, features), lambda i: (0, 0))
    whole = pl.BlockSpec((length, features), lambda i: (0, 0))
    tall = lambda k: pl.BlockSpec((features, columns), lambda i: (0, i + k * steps))
    return pl.pallas_call(
        feed_kernel,
        grid=(steps,),
        in_specs=[part] * 4 + [tall(0), tall(1), tall(2)],
        out_specs=[
            pl.BlockSpec((length, columns), lambda i: (0, i)),
            pl.BlockSpec((length, 2 * columns), lambda i: (0, i)),
            whole,
            whole,
            part,
            part,
        ],
        out_shape=[
            jax.ShapeDtypeStruct((length, width), BF),
            jax.ShapeDtypeStruct((length, 2 * width), BF),
        ]
        + [jax.ShapeDtypeStruct((length, features), BF)] * 2
        + [jax.ShapeDtypeStruct((rows, features), BF)] * 2,
        scratch_shapes=[pltpu.VMEM((length, features), F32)],
        compiler_params=pltpu.CompilerParams(vmem_limit_bytes=VMEM_LIMIT),
        cost_estimate=pl.CostEstimate(
            flops=8 * 10**9, bytes_accessed=18 * 10**6, transcendentals=10**6
        ),
        name="feed",
    )(*xs, *cs, w, w, w)


def feed_grads_kernel(steps, xa_ref, xb_ref, ca_ref, cb_ref, ba_ref, bb_ref, ha_ref, hb_ref, out_ref):
    step = pl.program_id(0)

    @pl.when(step < 2 * steps)
    def _():
        out_ref[...] = (dotf(xa_ref[...], ba_ref[...], TN) + dotf(xb_ref[...], bb_ref[...], TN)).astype(BF)

    @pl.when(step >= 2 * steps)
    def _():
        out_ref[...] = (dotf(ca_ref[...], ha_ref[...], TN) + dotf(cb_ref[...], hb_ref[...], TN)).astype(BF)


def feed_grads_of(xs, cs, backs, hiddens, columns):
    length, features = xs[0].shape
    width = hiddens[0].shape[1]
    steps = width // columns
    whole = pl.BlockSpec((length, features), lambda i: (0, 0))

    def back_at(i):
        i = jnp.minimum(i, 2 * steps - 1)
        return (0, (i % steps) * 2 + i // steps)

    back = pl.BlockSpec((length, columns), back_at)
    hidden = pl.BlockSpec((length, columns), lambda i: (0, jnp.maximum(i - 2 * steps, 0)))
    return pl.pallas_call(
        functools.partial(feed_grads_kernel, steps),
        grid=(3 * steps,),
        in_specs=[whole] * 4 + [back] * 2 + [hidden] * 2,
        out_specs=pl.BlockSpec((features, columns), lambda i: (0, i)),
        out_shape=jax.ShapeDtypeStruct((features, 3 * width), BF),
        compiler_params=pltpu.CompilerParams(vmem_limit_bytes=VMEM_LIMIT),
        cost_estimate=pl.CostEstimate(
            flops=12 * length * features * width,
            bytes_accessed=25 * 10**6,
            transcendentals=0,
        ),
        name="feed_grads",
    )(*xs, *cs, *backs, *hiddens)


def down_kernel(ha_ref, hb_ref, w_ref, *outs):
    rows = outs[0].shape[0]
    w = w_ref[...]
    for h_ref, (keep_ref, send_ref) in zip((ha_ref, hb_ref), (outs[:2], outs[2:])):
        part = dotf(h_ref[...], w, NT)
        keep_ref[...] = part[:rows].astype(BF)
        send_ref[...] = part[rows:].astype(BF)


def down_product(hiddens, w):
    length, width = hiddens[0].shape
    features = w.shape[0]
    hidden = pl.BlockSpec((length, width), lambda i: (0, 0))
    part = pl.BlockSpec((length // 2, features), lambda i: (0, 0))
    return pl.pallas_call(
        down_kernel,
        grid=(1,),
        in_specs=[hidden, hidden, pl.BlockSpec((features, width), lambda i: (0, 2))],
        out_specs=[part] * 4,
        out_shape=[jax.ShapeDtypeStruct((length // 2, features), BF)] * 4,
        compiler_params=pltpu.CompilerParams(vmem_limit_bytes=VMEM_LIMIT),
        cost_estimate=pl.CostEstimate(
            flops=4 * length * features * width, bytes_accessed=8 * 10**6, transcendentals=0
        ),
        name="down_product",
    )(*hiddens, w)


def pack_kernel(places, *refs):
    ins, out_ref = refs[:-1], refs[-1]
    for begin, ref in zip(places, ins):
        width = ref.shape[1]
        if width % 128:
            out_ref[:, begin : begin + 128] = jnp.zeros((out_ref.shape[0], 128), BF)
        out_ref[:, begin : begin + width] = ref[...].astype(BF)


def pack(parts, places, columns):
    rows = parts[0].shape[0]
    return pl.pallas_call(
        functools.partial(pack_kernel, places),
        out_shape=jax.ShapeDtypeStruct((rows, columns), BF),
        compiler_params=pltpu.CompilerParams(vmem_limit_bytes=VMEM_LIMIT),
        cost_estimate=pl.CostEstimate(
            flops=rows * columns, bytes_accessed=6 * rows * columns, transcendentals=0
        ),
        name="pack",
    )(*parts)


def attend_grads_kernel(
    place_ref, x_ref, m_ref, grad_ref, mixed_ref, keep_ref, send_ref, out_ref, gain_ref
):
    inner = grad_ref.shape[1]
    out_ref[:, :inner] = dotf(x_ref[...], grad_ref[...], TN).astype(BF)
    out_ref[:, inner:] = dotf(m_ref[...], mixed_ref[...], TN).astype(BF)
    block = x_ref.shape[0] // 4
    total = jnp.zeros((1, gain_ref.shape[1]), F32)
    for n, at in enumerate(starts(place_ref, block)):
        part = (send_ref if n >> 1 else keep_ref)[(n & 1) * block : ((n & 1) + 1) * block, :]
        own = x_ref[pl.ds(at, block), :].astype(F32) * part.astype(F32)
        total = total + jnp.sum(own, axis=0, keepdims=True)
    gain_ref[...] = jnp.broadcast_to(total, gain_ref.shape)


def attend_grads(place, x, m, grads, mixed, keep, send):
    length, features = x.shape
    columns = grads.shape[1] + mixed.shape[1]
    return pl.pallas_call(
        attend_grads_kernel,
        in_specs=in_memory(1, 6),
        out_shape=(
            jax.ShapeDtypeStruct((features, columns), BF),
            jax.ShapeDtypeStruct((8, features), F32),
        ),
        compiler_params=pltpu.CompilerParams(vmem_limit_bytes=VMEM_LIMIT),
        cost_estimate=pl.CostEstimate(
            flops=2 * length * features * columns, bytes_accessed=2 * 10**7, transcendentals=0
        ),
        name="attend_grads",
    )(place, x, m, grads, mixed, keep, send)


def finish_kernel(widths, odd_ref, low_ref, high_ref, a_ref, b_ref, c_ref, *out_refs):
    odd = odd_ref[0] == 1

    def put(first_ref, second_ref):
        begin = 0
        for width, out_ref in zip(widths, out_refs):
            first = first_ref[:, begin : begin + width].astype(F32)
            out_ref[...] = first + second_ref[:, begin : begin + width].astype(F32)
            begin += width

    @pl.when(odd)
    def _():
        put(c_ref, b_ref)

    @pl.when(jnp.logical_not(odd))
    def _():
        put(low_ref, a_ref)


def finish(odd, low, high, a, b, c, widths):
    rows = low.shape[0]
    return pl.pallas_call(
        functools.partial(finish_kernel, widths),
        in_specs=in_memory(1, 5),
        out_shape=[jax.ShapeDtypeStruct((rows, width), F32) for width in widths],
        compiler_params=pltpu.CompilerParams(vmem_limit_bytes=VMEM_LIMIT),
        cost_estimate=pl.CostEstimate(flops=10**6, bytes_accessed=8 * 10**6, transcendentals=0),
        name="finish",
    )(odd, low, high, a, b, c)


class Layout:
    def __init__(self, dp, tensor):
        self.groups = [[core + 2 * i for i in range(dp // 2)] for core in range(2)]
        self.core = [(d, d ^ 1) for d in range(dp)]
        self.pair = [(z, z ^ 1) for z in range(tensor)]
        flat = lambda d, z: d * tensor + z
        devices = [(d, z) for d in range(dp) for z in range(tensor)]
        away = [(d, z) for d, z in devices if (d & 1) != (z >> 1)]
        self.move = [(flat(d, z), flat(d ^ 1, z ^ 2)) for d, z in away]
        even = [(d, z) for d, z in devices if d & 1 == 0]
        odd = [(d, z) for d, z in devices if d & 1 == 1]
        self.even_far = [(flat(d, z), flat(d + 1, z ^ 2)) for d, z in even]
        self.odd_far = [(flat(d, z), flat(d, z ^ 2)) for d, z in odd]
        self.odd_even = [(flat(d, z), flat(d - 1, z)) for d, z in odd]
        self.back_even_far = [(b, a) for a, b in self.even_far]
        self.back_odd_even = [(b, a) for a, b in self.odd_even]


def cat(*parts):
    return jnp.concatenate(parts, axis=0)


def after(x, *deps):
    return lax.optimization_barrier((x, *deps))[0]


def swap_weight(lay, w, odd, *deps):
    a = lax.ppermute(w, BOTH, lay.even_far)
    b = lax.ppermute(w, BOTH, lay.odd_far)
    c = lax.ppermute(w, BOTH, lay.odd_even)
    return jnp.where(odd, cat(after(a, *deps), b), cat(w, c))


def gather_rows(lay, rows):
    return lax.all_gather(rows, "dp", axis=0, tiled=True, axis_index_groups=lay.groups)


def scatter_rows(lay, g):
    return lax.psum_scatter(
        g, "dp", scatter_dimension=0, tiled=True, axis_index_groups=lay.groups
    )


def share_grad(lay, r, odd, widths):
    half = r.shape[0] // 2
    low, high = r[:half], r[half:]
    a = lax.ppermute(low, BOTH, lay.back_even_far)
    b = lax.ppermute(high, BOTH, lay.odd_far)
    c = lax.ppermute(high, BOTH, lay.back_odd_even)
    return finish(odd.astype(jnp.int32).reshape(1), low, high, a, b, c, widths)


def gather_pair(lay, x, *deps):
    core = lax.ppermute(x, "dp", lay.core)
    z = lax.ppermute(x, "tensor", lay.pair)
    return x, z, core, lax.ppermute(after(z, *deps), "dp", lay.core)


def scatter_core(lay, keep, send):
    got = lax.ppermute(send, "dp", lay.core)
    half = keep.shape[0] // 2
    mine = keep[:half].astype(F32) + got[:half].astype(F32)
    other = keep[half:].astype(F32) + got[half:].astype(F32)
    return mine, other.astype(BF)


def scatter_z(lay, mine, other):
    return mine + lax.ppermute(other, "tensor", lay.pair).astype(F32)


def sum_all(x, axis):
    size = lax.axis_size(axis)
    step = 1
    while step < size:
        x = x + lax.ppermute(x, axis, [(i, i ^ step) for i in range(size)])
        step *= 2
    return x


def inverse_rms(rows):
    return lax.rsqrt(jnp.mean(rows * rows, axis=-1, keepdims=True) + EPS)


def norm_back(rows, gain, grad):
    r = inverse_rms(rows)
    xhat = rows * r
    scaled = grad * gain
    return r * (scaled - xhat * jnp.mean(scaled * xhat, axis=-1, keepdims=True))


def per_device(
    layer_input,
    segment_ids,
    attn_gain,
    query_weight,
    key_weight,
    value_weight,
    forget_weight,
    forget_bias,
    output_weight,
    feed_gain,
    gate_weight,
    up_weight,
    down_weight,
    output_cotangent,
):
    lay = Layout(lax.axis_size("dp"), lax.axis_size("tensor"))
    z = lax.axis_index("tensor")
    odd = (lax.axis_index("dp") & 1) == 1
    zodd = (z & 1) == 1
    away = odd != (z >= 2)
    quarter = jnp.where(odd, z ^ 2, z)
    heads = forget_weight.shape[1]
    width = query_weight.shape[1]
    hidden_width = gate_weight.shape[1]
    features = layer_input.shape[1]
    place = jnp.stack([odd, zodd]).astype(jnp.int32)

    def moved(x):
        return jnp.where(away, lax.ppermute(x, BOTH, lay.move), x)

    def moved_back(x):
        low = lax.ppermute(x.astype(BF), BOTH, lay.move)
        return jnp.where(away, low.astype(F32), x)

    w_attn_local = pack(
        [query_weight, key_weight, value_weight, forget_weight, output_weight],
        [0, width, 2 * width, 3 * width, 3 * width + 128],
        4 * width + 128,
    )
    attn_rows = swap_weight(lay, w_attn_local, odd)
    w_attn = gather_rows(lay, attn_rows)
    w_feed_local = pack(
        [gate_weight, up_weight, down_weight],
        [0, hidden_width, 2 * hidden_width],
        3 * hidden_width,
    )
    feed_rows = swap_weight(lay, after(w_feed_local, attn_rows), odd)
    w_feed = gather_rows(lay, feed_rows)
    segment = jnp.where(
        away, lax.ppermute(after(segment_ids, attn_rows), "dp", lay.core), segment_ids
    )
    seg_row = segment[None, :]
    bias = jnp.pad(
        lax.dynamic_slice_in_dim(forget_bias, quarter * heads, heads), (0, 128 - heads)
    )[None, :]

    layer = moved_back(after(layer_input, feed_rows))
    normed = (layer * inverse_rms(layer) * attn_gain).astype(BF)
    xs = gather_pair(lay, normed)
    cot_low = moved(after(output_cotangent.astype(BF), normed))
    cot_z = lax.ppermute(after(cot_low, xs[1]), "tensor", lay.pair)
    attn_normed, qkv, mixed, keep, send, rows, decay, closed = attend(
        place, (*xs[:3], after(xs[3], cot_low)), w_attn, bias, seg_row, heads
    )
    mine, other = scatter_core(lay, keep, after(send, cot_z))
    cot_core = lax.ppermute(after(cot_low, other), "dp", lay.core)
    cot_core_z = lax.ppermute(after(cot_z, other), "dp", lay.core)
    branch = scatter_z(lay, mine, other)
    middle = layer + branch

    feed_local = (middle * inverse_rms(middle) * feed_gain).astype(BF)
    feed_z = lax.ppermute(feed_local, "tensor", lay.pair)
    feed_core = lax.ppermute(feed_local, "dp", lay.core)
    hidden_a, back_a, x_a, c_a, keep_a, send_a = feed(
        (feed_local, feed_core), (cot_low, cot_core), w_feed, 512
    )
    feed_z = after(feed_z, keep_a)
    feed_core_z = lax.ppermute(feed_z, "dp", lay.core)
    hidden_b, back_b, x_b, c_b, keep_b, send_b = feed(
        (feed_z, feed_core_z), (cot_z, cot_core_z), w_feed, 512
    )
    got_a = lax.ppermute(send_a, "dp", lay.core)
    got_b = lax.ppermute(send_b, "dp", lay.core)
    other = (keep_b.astype(F32) + got_b.astype(F32)).astype(BF)
    got_z = lax.ppermute(other, "tensor", lay.pair)
    hidden_b, other = lax.optimization_barrier((hidden_b, other))
    feed_grads = feed_grads_of(
        (x_a, x_b), (c_a, c_b), (back_a, back_b), (hidden_a, hidden_b), 512
    )
    feed_scattered = scatter_rows(lay, feed_grads)
    feed_normed_grad = keep_a.astype(F32) + got_a.astype(F32) + got_z.astype(F32)
    feed_normed_grad = after(feed_normed_grad, feed_grads)

    middle_part = norm_back(middle, feed_gain, feed_normed_grad)
    cotangent = jnp.where(away, cot_low.astype(F32), output_cotangent)
    middle_low = (cotangent + middle_part).astype(BF)
    ms = gather_pair(lay, middle_low)
    down_keep_a, down_send_a, down_keep_b, down_send_b = down_product(
        (hidden_a, after(hidden_b, middle_low)), w_feed
    )
    got_b = lax.ppermute(down_send_b, "dp", lay.core)
    other = (down_keep_b.astype(F32) + got_b.astype(F32)).astype(BF)
    got_a = lax.ppermute(down_send_a, "dp", lay.core)
    ms = (*ms[:3], after(ms[3], other))
    feed_gain_part = sum(
        jnp.sum(part.astype(F32) * x.astype(F32), axis=0)
        for part, x in (
            (after(keep_a, middle_low), x_a[: keep_a.shape[0]]),
            (send_a, x_a[keep_a.shape[0] :]),
            (keep_b, x_b[: keep_b.shape[0]]),
            (send_b, x_b[keep_b.shape[0] :]),
        )
    )
    feed_gain_part = feed_gain_part / feed_gain

    middle_all, grads, keep, send, bias_part = attend_back(
        place, ms, w_attn, qkv, mixed, rows, decay, closed, seg_row, heads
    )
    down = branch + down_keep_a.astype(F32) + got_a.astype(F32)
    down = down + after(lax.ppermute(other, "tensor", lay.pair), bias_part).astype(F32)
    down_back = moved_back(down)
    attn_grads, attn_gain_part = attend_grads(
        place, attn_normed, middle_all, after(grads, down), mixed, keep, send
    )
    layer_output = layer_input + down_back
    bias_full = lax.dynamic_update_slice_in_dim(
        jnp.zeros(forget_bias.shape, F32), bias_part[0, :heads], quarter * heads, 0
    )
    packed = cat(attn_gain_part[0] / attn_gain, feed_gain_part, bias_full)
    size = packed.shape[0]
    packed = jnp.pad(packed, (0, -size % 1024)).reshape(-1, 128)
    packed = sum_all(after(packed, down_back), "tensor")
    attn_scattered = scatter_rows(lay, after(attn_grads, feed_scattered, packed))
    small = sum_all(after(packed, attn_grads), "dp").reshape(-1)
    gate_shard, up_shard, down_shard = share_grad(
        lay, after(feed_scattered, small), odd, [hidden_width] * 3
    )
    mine, other = scatter_core(lay, keep, after(send, packed))
    attn_normed_grad = scatter_z(lay, mine, other)
    input_part = norm_back(layer, attn_gain, attn_normed_grad)
    input_back = moved_back(after(middle_part + input_part, gate_shard))
    input_grad = output_cotangent + input_back

    query_shard, key_shard, value_shard, forget_shard, output_shard = share_grad(
        lay,
        after(attn_scattered, small, gate_shard),
        odd,
        [width, width, width, 128, width],
    )
    return (
        layer_output,
        input_grad,
        small[:features],
        query_shard,
        key_shard,
        value_shard,
        forget_shard[:, :heads],
        small[2 * features : size],
        output_shard,
        small[features : 2 * features],
        gate_shard,
        up_shard,
        down_shard,
    )


def solution(mesh):
    tokens = P(("dp", "tensor"), None)
    weight = P("dp", "tensor")
    in_specs = (
        tokens, P("dp"), P(), weight, weight, weight, weight, P(), weight, P(), weight, weight, weight, tokens,
    )
    out_specs = (
        tokens, tokens, P(), weight, weight, weight, weight, P(), weight, P(), weight, weight, weight,
    )
    return jax.shard_map(
        per_device, mesh=mesh, in_specs=in_specs, out_specs=out_specs, check_vma=False
    )
```

```python
import functools

import jax
import jax.numpy as jnp
from jax import lax
from jax.experimental import pallas as pl
from jax.experimental.pallas import tpu as pltpu
from jax.sharding import PartitionSpec as P

F32 = jnp.float32
BF = jnp.bfloat16
NT = (((1,), (1,)), ((), ()))
NN = (((1,), (0,)), ((), ()))
TN = (((0,), (0,)), ((), ()))
BOTH = ("dp", "tensor")
EPS = 1e-6


def dotf(a, b, dn):
    return lax.dot_general(a, b, dn, preferred_element_type=F32)


MIB = 1024 * 1024
VMEM_LIMIT = 60 * MIB


def split3(x):
    a = x.astype(BF)
    r = x - a.astype(F32)
    b = r.astype(BF)
    return a, b, (r - b.astype(F32)).astype(BF)


def exact_dot(left, right, dims):
    return sum(dotf(left, part, dims) for part in split3(right))


def column_of(row):
    parts = [
        jnp.broadcast_to(row[:, i : i + 128], (128, 128)).T[:, :1]
        for i in range(0, row.shape[1], 128)
    ]
    return jnp.concatenate(parts, axis=0)


def starts(place_ref, block):
    odd, zodd = place_ref[0], place_ref[1]
    return [
        pl.multiple_of(
            ((1 - odd if k >> 1 else odd) * 2 + (1 - zodd if k & 1 else zodd)) * block, block
        )
        for k in range(4)
    ]


def attend_kernel(
    heads, span, place_ref, x0_ref, x1_ref, x2_ref, x3_ref, w_ref, bias_ref, seg_ref, x_ref, qkv_ref, mixed_ref, keep_ref, send_ref, rows_ref, decay_ref, closed_ref, stat_ref, drow_ref, own_ref
):
    length = x_ref.shape[0]
    block = length // 4
    width = heads * 64
    places = starts(place_ref, block)
    for at, part_ref in zip(places, (x0_ref, x1_ref, x2_ref, x3_ref)):
        x_ref[pl.ds(at, block), :] = part_ref[...]
    x = x_ref[...]
    qkv_ref[...] = dotf(x, w_ref[:, : 3 * width], NN).astype(BF)
    logits = dotf(x, w_ref[:, 3 * width : 3 * width + 128], NN) + bias_ref[...]
    small = jnp.exp(-jnp.abs(logits))
    log_decay = -(jnp.maximum(-logits, 0.0) + jnp.log1p(small))
    closed_ref[...] = jnp.where(logits >= 0, small, 1.0) / (1.0 + small)
    i = lax.broadcasted_iota(jnp.int32, (128, 128), 0)
    j = lax.broadcasted_iota(jnp.int32, (128, 128), 1)
    below = (i >= j).astype(BF)
    carry = jnp.zeros((1, 128), F32)
    for b in range(0, length, 128):
        total = exact_dot(below, log_decay[b : b + 128], NN) + carry
        decay_ref[b : b + 128, :] = total
        drow_ref[:, b : b + 128] = total.T
        carry = total[127:128]
    lane = lax.broadcasted_iota(jnp.int32, (1, 128), 1)
    i = lax.broadcasted_iota(jnp.int32, (span, span), 0)
    j = lax.broadcasted_iota(jnp.int32, (span, span), 1)
    causal = i >= j
    seg = seg_ref[...]
    for pair in range(heads // 2):
        at = pair * 128
        for begin in range(0, length, span):
            end = begin + span
            q = qkv_ref[begin:end, at : at + 128].astype(F32) * 0.125
            k = qkv_ref[:end, width + at : width + at + 128]
            v = qkv_ref[:end, 2 * width + at : 2 * width + at + 128]
            same = column_of(seg[:, begin:end]) == seg[:, :end]
            outs = []
            for side in range(2):
                h = 2 * pair + side
                own = (lane >= 64) if side else (lane < 64)
                s = dotf(jnp.where(own, q, 0.0).astype(BF), k, NT)
                s = s + decay_ref[begin:end, h : h + 1] - drow_ref[h : h + 1, :end]
                s = jnp.where(same, s, -1e30)
                last = jnp.where(causal, s[:, begin:], -1e30)
                s = jnp.concatenate([s[:, :begin], last], axis=1) if begin else last
                highest = jnp.max(s, axis=1, keepdims=True)
                p = jnp.exp(s - highest)
                total = jnp.sum(p, axis=1, keepdims=True)
                outs.append(dotf(p.astype(BF), v, NN) / total)
                stat_ref[begin:end, h : h + 1] = highest + jnp.log(total)
            mixed_ref[begin:end, at : at + 128] = jnp.where(lane < 64, *outs).astype(BF)
    rows_ref[0:8, :] = drow_ref[0:8, :]
    for b in range(0, length, 128):
        rows_ref[8:16, b : b + 128] = stat_ref[b : b + 128, :].T[0:8]
    for n, at in enumerate(places):
        own_ref[n * block : (n + 1) * block, :] = mixed_ref[pl.ds(at, block), :]
    branch = dotf(own_ref[...], w_ref[:, 3 * width + 128 :], NT)
    keep_ref[...] = branch[: 2 * block].astype(BF)
    send_ref[...] = branch[2 * block :].astype(BF)


def in_memory(scalars, arrays):
    return [pl.BlockSpec(memory_space=pltpu.SMEM)] * scalars + [
        pl.BlockSpec(memory_space=pltpu.VMEM)
    ] * arrays


def attend(place, xs, w, bias, seg, heads):
    block, features = xs[0].shape
    length = 4 * block
    width = heads * 64
    return pl.pallas_call(
        functools.partial(attend_kernel, heads, 256),
        in_specs=in_memory(1, 7),
        out_shape=(
            jax.ShapeDtypeStruct((length, features), BF),
            jax.ShapeDtypeStruct((length, 3 * width), BF),
            jax.ShapeDtypeStruct((length, width), BF),
            jax.ShapeDtypeStruct((length // 2, features), BF),
            jax.ShapeDtypeStruct((length // 2, features), BF),
            jax.ShapeDtypeStruct((16, length), F32),
            jax.ShapeDtypeStruct((length, 128), F32),
            jax.ShapeDtypeStruct((length, 128), F32),
        ),
        scratch_shapes=[
            pltpu.VMEM((length, 128), F32),
            pltpu.VMEM((128, length), F32),
            pltpu.VMEM((length, width), BF),
        ],
        compiler_params=pltpu.CompilerParams(vmem_limit_bytes=38 * MIB),
        cost_estimate=pl.CostEstimate(
            flops=12 * 10**9, bytes_accessed=2 * 10**7, transcendentals=5 * 10**6
        ),
        name="attend",
    )(place, *xs, w, bias, seg)


def attend_back_kernel(
    heads, span, place_ref, m0_ref, m1_ref, m2_ref, m3_ref, w_ref, qkv_ref, mixed_ref, rows_ref, decay_ref, closed_ref, seg_ref, m_ref, grad_ref, keep_ref, send_ref, bias_ref, mb_ref, dq_ref, sums_ref, drow_ref, own_ref
):
    length = m_ref.shape[0]
    block = length // 4
    width = heads * 64
    places = starts(place_ref, block)
    for at, part_ref in zip(places, (m0_ref, m1_ref, m2_ref, m3_ref)):
        m_ref[pl.ds(at, block), :] = part_ref[...]
    mb_ref[...] = dotf(m_ref[...], w_ref[:, 3 * width + 128 :], NN).astype(BF)
    lane = lax.broadcasted_iota(jnp.int32, (1, 128), 1)
    i = lax.broadcasted_iota(jnp.int32, (span, span), 0)
    j = lax.broadcasted_iota(jnp.int32, (span, span), 1)
    causal = i <= j
    seg = seg_ref[...]
    sums_ref[...] = jnp.zeros_like(sums_ref)
    drow_ref[...] = jnp.zeros_like(drow_ref)
    side_row = lax.broadcasted_iota(jnp.int32, (8, 128), 0)
    side_lane = lax.broadcasted_iota(jnp.int32, (8, 128), 1)
    chosen = ((side_lane // 64) == side_row).astype(BF)
    for pair in range(heads // 2):
        at = pair * 128
        own_product = mb_ref[:, at : at + 128].astype(F32) * mixed_ref[:, at : at + 128].astype(F32)
        delta = exact_dot(chosen, own_product, NT)
        for begin in range(0, length, span):
            end = begin + span
            k = qkv_ref[begin:end, width + at : width + at + 128]
            v = qkv_ref[begin:end, 2 * width + at : 2 * width + at + 128]
            q = qkv_ref[begin:, at : at + 128]
            mb = mb_ref[begin:, at : at + 128]
            same = column_of(seg[:, begin:end]) == seg[:, begin:]
            dks, dvs, dqs = [], [], []
            for side in range(2):
                h = 2 * pair + side
                own = (lane >= 64) if side else (lane < 64)
                own_k = jnp.where(own, k.astype(F32) * 0.125, 0.0).astype(BF)
                own_v = jnp.where(own, v.astype(F32), 0.0).astype(BF)
                s = dotf(own_k, q, NT)
                s = s + (rows_ref[h : h + 1, begin:] - rows_ref[8 + h : 9 + h, begin:])
                s = jnp.where(same, s - decay_ref[begin:end, h : h + 1], -1e30)
                first = jnp.where(causal, s[:, :span], -1e30)
                s = jnp.concatenate([first, s[:, span:]], axis=1) if end < length else first
                p = jnp.exp(s)
                dvs.append(dotf(p.astype(BF), mb, NN))
                ds = p * (dotf(own_v, mb, NT) - delta[side : side + 1, begin:])
                ds_low = (ds * 0.125).astype(BF)
                dks.append(dotf(ds_low, q, NN))
                dqs.append(dotf(ds_low, k, TN))
                sums_ref[begin:end, h : h + 1] = jnp.sum(ds, axis=1, keepdims=True)
                drow_ref[h : h + 1, begin:] += jnp.sum(ds, axis=0, keepdims=True)
            k_at, v_at = width + at, 2 * width + at
            grad_ref[begin:end, k_at : k_at + 128] = jnp.where(lane < 64, *dks).astype(BF)
            grad_ref[begin:end, v_at : v_at + 128] = jnp.where(lane < 64, *dvs).astype(BF)
            dq = jnp.where(lane < 64, *dqs)
            if begin:
                dq_ref[begin:, :] += dq
            else:
                dq_ref[...] = dq
        grad_ref[:, at : at + 128] = dq_ref[...].astype(BF)
    i = lax.broadcasted_iota(jnp.int32, (128, 128), 0)
    j = lax.broadcasted_iota(jnp.int32, (128, 128), 1)
    above = (i <= j).astype(BF)
    carry = jnp.zeros((1, 128), F32)
    bias = jnp.zeros((1, 128), F32)
    blank = jnp.zeros((120, 128), F32)
    for b in reversed(range(0, length, 128)):
        row_sum = jnp.concatenate([drow_ref[:, b : b + 128], blank], axis=0).T
        total = exact_dot(above, row_sum - sums_ref[b : b + 128, :], NN) + carry
        carry = total[0:1]
        back = (closed_ref[b : b + 128, :] * total).astype(BF)
        grad_ref[b : b + 128, 3 * width :] = back
        bias = bias + jnp.sum(back.astype(F32), axis=0, keepdims=True)
    bias_ref[...] = jnp.broadcast_to(bias, bias_ref.shape)
    for n, at in enumerate(places):
        own_ref[n * block : (n + 1) * block, :] = grad_ref[pl.ds(at, block), :]
    part = dotf(own_ref[...], w_ref[:, : 3 * width + 128], NT)
    keep_ref[...] = part[: 2 * block].astype(BF)
    send_ref[...] = part[2 * block :].astype(BF)


def attend_back(place, ms, w, qkv, mixed, rows, decay, closed, seg, heads):
    block, features = ms[0].shape
    length = 4 * block
    width = heads * 64
    return pl.pallas_call(
        functools.partial(attend_back_kernel, heads, 256),
        in_specs=in_memory(1, 11),
        out_shape=(
            jax.ShapeDtypeStruct((length, features), BF),
            jax.ShapeDtypeStruct((length, 3 * width + 128), BF),
            jax.ShapeDtypeStruct((length // 2, features), BF),
            jax.ShapeDtypeStruct((length // 2, features), BF),
            jax.ShapeDtypeStruct((8, 128), F32),
        ),
        scratch_shapes=[
            pltpu.VMEM((length, width), BF),
            pltpu.VMEM((length, 128), F32),
            pltpu.VMEM((length, 128), F32),
            pltpu.VMEM((8, length), F32),
            pltpu.VMEM((length, 3 * width + 128), BF),
        ],
        compiler_params=pltpu.CompilerParams(vmem_limit_bytes=38 * MIB),
        cost_estimate=pl.CostEstimate(
            flops=150 * 10**9, bytes_accessed=2 * 10**7, transcendentals=5 * 10**6
        ),
        name="attend_back",
    )(place, *ms, w, qkv, mixed, rows, decay, closed, seg)


def feed_kernel(*refs):
    x_parts, c_parts = refs[:2], refs[2:4]
    wg_ref, wu_ref, wd_ref, hidden_ref, back_ref, x_ref, c_ref, keep_ref, send_ref, total_ref = refs[4:]
    step = pl.program_id(0)
    block = x_ref.shape[0] // 2
    columns = wg_ref.shape[1]

    @pl.when(step == 0)
    def _():
        for n in range(2):
            x_ref[n * block : (n + 1) * block, :] = x_parts[n][...]
            c_ref[n * block : (n + 1) * block, :] = c_parts[n][...]

    x = x_ref[...]
    wg, wu = wg_ref[...], wu_ref[...]
    gate = dotf(x, wg, NN)
    up = dotf(x, wu, NN)
    back = dotf(c_ref[...], wd_ref[...], NN)
    sig = 1.0 / (1.0 + jnp.exp(-gate))
    silu = gate * sig
    hidden_ref[...] = (silu * up).astype(BF)
    back_ref[:, :columns] = (back * up * sig * (1.0 + gate * (1.0 - sig))).astype(BF)
    back_ref[:, columns:] = (back * silu).astype(BF)
    part = dotf(back_ref[...], jnp.concatenate([wg, wu], axis=1), NT)

    @pl.when(step == 0)
    def _():
        total_ref[...] = part

    @pl.when((step > 0) & (step < pl.num_programs(0) - 1))
    def _():
        total_ref[...] += part

    @pl.when(step == pl.num_programs(0) - 1)
    def _():
        keep_ref[...] = (total_ref[:block] + part[:block]).astype(BF)
        send_ref[...] = (total_ref[block:] + part[block:]).astype(BF)


def feed(xs, cs, w, columns):
    rows, features = xs[0].shape
    length = 2 * rows
    width = w.shape[1] // 3
    steps = width // columns
    part = pl.BlockSpec((rows, features), lambda i: (0, 0))
    whole = pl.BlockSpec((length, features), lambda i: (0, 0))
    tall = lambda k: pl.BlockSpec((features, columns), lambda i: (0, i + k * steps))
    return pl.pallas_call(
        feed_kernel,
        grid=(steps,),
        in_specs=[part] * 4 + [tall(0), tall(1), tall(2)],
        out_specs=[
            pl.BlockSpec((length, columns), lambda i: (0, i)),
            pl.BlockSpec((length, 2 * columns), lambda i: (0, i)),
            whole,
            whole,
            part,
            part,
        ],
        out_shape=[
            jax.ShapeDtypeStruct((length, width), BF),
            jax.ShapeDtypeStruct((length, 2 * width), BF),
        ]
        + [jax.ShapeDtypeStruct((length, features), BF)] * 2
        + [jax.ShapeDtypeStruct((rows, features), BF)] * 2,
        scratch_shapes=[pltpu.VMEM((length, features), F32)],
        compiler_params=pltpu.CompilerParams(vmem_limit_bytes=38 * MIB),
        cost_estimate=pl.CostEstimate(
            flops=8 * 10**9, bytes_accessed=18 * 10**6, transcendentals=10**6
        ),
        name="feed",
    )(*xs, *cs, w, w, w)


def feed_grads_kernel(steps, xa_ref, xb_ref, ca_ref, cb_ref, ba_ref, bb_ref, ha_ref, hb_ref, out_ref):
    step = pl.program_id(0)

    @pl.when(step < 2 * steps)
    def _():
        out_ref[...] = (dotf(xa_ref[...], ba_ref[...], TN) + dotf(xb_ref[...], bb_ref[...], TN)).astype(BF)

    @pl.when(step >= 2 * steps)
    def _():
        out_ref[...] = (dotf(ca_ref[...], ha_ref[...], TN) + dotf(cb_ref[...], hb_ref[...], TN)).astype(BF)


def feed_grads_of(xs, cs, backs, hiddens, columns):
    length, features = xs[0].shape
    width = hiddens[0].shape[1]
    steps = width // columns
    whole = pl.BlockSpec((length, features), lambda i: (0, 0))

    def back_at(i):
        i = jnp.minimum(i, 2 * steps - 1)
        return (0, (i % steps) * 2 + i // steps)

    back = pl.BlockSpec((length, columns), back_at)
    hidden = pl.BlockSpec((length, columns), lambda i: (0, jnp.maximum(i - 2 * steps, 0)))
    return pl.pallas_call(
        functools.partial(feed_grads_kernel, steps),
        grid=(3 * steps,),
        in_specs=[whole] * 4 + [back] * 2 + [hidden] * 2,
        out_specs=pl.BlockSpec((features, columns), lambda i: (0, i)),
        out_shape=jax.ShapeDtypeStruct((features, 3 * width), BF),
        compiler_params=pltpu.CompilerParams(vmem_limit_bytes=38 * MIB),
        cost_estimate=pl.CostEstimate(
            flops=12 * length * features * width,
            bytes_accessed=25 * 10**6,
            transcendentals=0,
        ),
        name="feed_grads",
    )(*xs, *cs, *backs, *hiddens)


def down_kernel(ha_ref, hb_ref, w_ref, *outs):
    rows = outs[0].shape[0]
    w = w_ref[...]
    for h_ref, (keep_ref, send_ref) in zip((ha_ref, hb_ref), (outs[:2], outs[2:])):
        part = dotf(h_ref[...], w, NT)
        keep_ref[...] = part[:rows].astype(BF)
        send_ref[...] = part[rows:].astype(BF)


def down_product(hiddens, w):
    length, width = hiddens[0].shape
    features = w.shape[0]
    hidden = pl.BlockSpec((length, width), lambda i: (0, 0))
    part = pl.BlockSpec((length // 2, features), lambda i: (0, 0))
    return pl.pallas_call(
        down_kernel,
        grid=(1,),
        in_specs=[hidden, hidden, pl.BlockSpec((features, width), lambda i: (0, 2))],
        out_specs=[part] * 4,
        out_shape=[jax.ShapeDtypeStruct((length // 2, features), BF)] * 4,
        compiler_params=pltpu.CompilerParams(vmem_limit_bytes=38 * MIB),
        cost_estimate=pl.CostEstimate(
            flops=4 * length * features * width, bytes_accessed=8 * 10**6, transcendentals=0
        ),
        name="down_product",
    )(*hiddens, w)


def unit(rows, columns):
    i = lax.broadcasted_iota(jnp.int32, (rows, columns), 0)
    j = lax.broadcasted_iota(jnp.int32, (rows, columns), 1)
    return (i == j).astype(BF)


def pack_kernel(places, *refs):
    ins, out_ref = refs[:-1], refs[-1]
    for begin, ref in zip(places, ins):
        if ref.shape[0] == out_ref.shape[0]:
            out_ref[:, begin : begin + ref.shape[1]] = ref[...].astype(BF)
        else:
            turned = dotf(ref[...].astype(BF), unit(ref.shape[0], 128), TN)
            out_ref[:, begin : begin + 128] = turned.astype(BF)


def pack(parts, places, columns):
    rows = parts[-1].shape[0]
    return pl.pallas_call(
        functools.partial(pack_kernel, places),
        out_shape=jax.ShapeDtypeStruct((rows, columns), BF),
        compiler_params=pltpu.CompilerParams(vmem_limit_bytes=VMEM_LIMIT),
        cost_estimate=pl.CostEstimate(
            flops=rows * columns, bytes_accessed=6 * rows * columns, transcendentals=0
        ),
        name="pack",
    )(*parts)


def attend_grads_kernel(
    place_ref, x_ref, m_ref, grad_ref, mixed_ref, keep_ref, send_ref, out_ref, gain_ref
):
    inner = grad_ref.shape[1]
    out_ref[:, :inner] = dotf(x_ref[...], grad_ref[...], TN).astype(BF)
    out_ref[:, inner:] = dotf(m_ref[...], mixed_ref[...], TN).astype(BF)
    block = x_ref.shape[0] // 4
    total = jnp.zeros((1, gain_ref.shape[1]), F32)
    for n, at in enumerate(starts(place_ref, block)):
        part = (send_ref if n >> 1 else keep_ref)[(n & 1) * block : ((n & 1) + 1) * block, :]
        own = x_ref[pl.ds(at, block), :].astype(F32) * part.astype(F32)
        total = total + jnp.sum(own, axis=0, keepdims=True)
    gain_ref[...] = jnp.broadcast_to(total, gain_ref.shape)


def attend_grads(place, x, m, grads, mixed, keep, send):
    length, features = x.shape
    columns = grads.shape[1] + mixed.shape[1]
    return pl.pallas_call(
        attend_grads_kernel,
        in_specs=in_memory(1, 6),
        out_shape=(
            jax.ShapeDtypeStruct((features, columns), BF),
            jax.ShapeDtypeStruct((8, features), F32),
        ),
        compiler_params=pltpu.CompilerParams(vmem_limit_bytes=38 * MIB),
        cost_estimate=pl.CostEstimate(
            flops=2 * length * features * columns, bytes_accessed=2 * 10**7, transcendentals=0
        ),
        name="attend_grads",
    )(place, x, m, grads, mixed, keep, send)


def finish_kernel(widths, odd_ref, low_ref, high_ref, a_ref, b_ref, c_ref, *out_refs):
    odd = odd_ref[0] == 1

    def put(first_ref, second_ref):
        begin = 0
        for width, out_ref in zip(widths, out_refs):
            if width > 0:
                first = first_ref[:, begin : begin + width].astype(F32)
                out_ref[...] = first + second_ref[:, begin : begin + width].astype(F32)
            else:
                width = 128
                pick = unit(out_ref.shape[0], 128)
                out_ref[...] = dotf(pick, first_ref[:, begin : begin + 128], NT) + dotf(
                    pick, second_ref[:, begin : begin + 128], NT
                )
            begin += width

    @pl.when(odd)
    def _():
        put(c_ref, b_ref)

    @pl.when(jnp.logical_not(odd))
    def _():
        put(low_ref, a_ref)


def finish(odd, low, high, a, b, c, widths):
    rows = low.shape[0]
    return pl.pallas_call(
        functools.partial(finish_kernel, widths),
        in_specs=in_memory(1, 5),
        out_shape=[
            jax.ShapeDtypeStruct((rows, width) if width > 0 else (-width, rows), F32)
            for width in widths
        ],
        compiler_params=pltpu.CompilerParams(vmem_limit_bytes=38 * MIB),
        cost_estimate=pl.CostEstimate(flops=10**6, bytes_accessed=8 * 10**6, transcendentals=0),
        name="finish",
    )(odd, low, high, a, b, c)


class Layout:
    def __init__(self, dp, tensor):
        self.groups = [[core + 2 * i for i in range(dp // 2)] for core in range(2)]
        self.core = [(d, d ^ 1) for d in range(dp)]
        self.pair = [(z, z ^ 1) for z in range(tensor)]
        flat = lambda d, z: d * tensor + z
        devices = [(d, z) for d in range(dp) for z in range(tensor)]
        away = [(d, z) for d, z in devices if (d & 1) != (z >> 1)]
        self.move = [(flat(d, z), flat(d ^ 1, z ^ 2)) for d, z in away]
        even = [(d, z) for d, z in devices if d & 1 == 0]
        odd = [(d, z) for d, z in devices if d & 1 == 1]
        self.even_far = [(flat(d, z), flat(d + 1, z ^ 2)) for d, z in even]
        self.odd_far = [(flat(d, z), flat(d, z ^ 2)) for d, z in odd]
        self.odd_even = [(flat(d, z), flat(d - 1, z)) for d, z in odd]
        self.back_even_far = [(b, a) for a, b in self.even_far]
        self.back_odd_even = [(b, a) for a, b in self.odd_even]


def cat(*parts):
    return jnp.concatenate(parts, axis=0)


def after(x, *deps):
    return lax.optimization_barrier((x, *deps))[0]


def swap_weight(lay, w, odd, *deps):
    a = lax.ppermute(w, BOTH, lay.even_far)
    b = lax.ppermute(w, BOTH, lay.odd_far)
    c = lax.ppermute(w, BOTH, lay.odd_even)
    return jnp.where(odd, cat(after(a, *deps), b), cat(w, c))


def gather_rows(lay, rows):
    return lax.all_gather(rows, "dp", axis=0, tiled=True, axis_index_groups=lay.groups)


def scatter_rows(lay, g):
    return lax.psum_scatter(
        g, "dp", scatter_dimension=0, tiled=True, axis_index_groups=lay.groups
    )


def share_grad(lay, r, odd, widths):
    half = r.shape[0] // 2
    low, high = r[:half], r[half:]
    a = lax.ppermute(low, BOTH, lay.back_even_far)
    b = lax.ppermute(high, BOTH, lay.odd_far)
    c = lax.ppermute(high, BOTH, lay.back_odd_even)
    return finish(odd.astype(jnp.int32).reshape(1), low, high, a, b, c, widths)


def gather_pair(lay, x, *deps):
    core = lax.ppermute(x, "dp", lay.core)
    z = lax.ppermute(x, "tensor", lay.pair)
    return x, z, core, lax.ppermute(after(z, *deps), "dp", lay.core)


def scatter_core(lay, keep, send):
    got = lax.ppermute(send, "dp", lay.core)
    half = keep.shape[0] // 2
    mine = keep[:half].astype(F32) + got[:half].astype(F32)
    other = keep[half:].astype(F32) + got[half:].astype(F32)
    return mine, other.astype(BF)


def scatter_z(lay, mine, other):
    return mine + lax.ppermute(other, "tensor", lay.pair).astype(F32)


def sum_all(x, axis):
    size = lax.axis_size(axis)
    step = 1
    while step < size:
        x = x + lax.ppermute(x, axis, [(i, i ^ step) for i in range(size)])
        step *= 2
    return x


def inverse_rms(rows):
    return lax.rsqrt(jnp.mean(rows * rows, axis=-1, keepdims=True) + EPS)


def norm_back(rows, gain, grad):
    r = inverse_rms(rows)
    xhat = rows * r
    scaled = grad * gain
    return r * (scaled - xhat * jnp.mean(scaled * xhat, axis=-1, keepdims=True))


def per_device(
    layer_input,
    segment_ids,
    attn_gain,
    query_weight,
    key_weight,
    value_weight,
    forget_weight,
    forget_bias,
    output_weight,
    feed_gain,
    gate_weight,
    up_weight,
    down_weight,
    output_cotangent,
):
    lay = Layout(lax.axis_size("dp"), lax.axis_size("tensor"))
    z = lax.axis_index("tensor")
    odd = (lax.axis_index("dp") & 1) == 1
    zodd = (z & 1) == 1
    away = odd != (z >= 2)
    quarter = jnp.where(odd, z ^ 2, z)
    heads = forget_weight.shape[1]
    width = query_weight.shape[1]
    hidden_width = gate_weight.shape[1]
    features = layer_input.shape[1]
    place = jnp.stack([odd, zodd]).astype(jnp.int32)

    def moved(x):
        return jnp.where(away, lax.ppermute(x, BOTH, lay.move), x)

    def moved_back(x):
        low = lax.ppermute(x.astype(BF), BOTH, lay.move)
        return jnp.where(away, low.astype(F32), x)

    w_attn_local = pack(
        [query_weight, key_weight, value_weight, forget_weight.T, output_weight],
        [0, width, 2 * width, 3 * width, 3 * width + 128],
        4 * width + 128,
    )
    attn_rows = swap_weight(lay, w_attn_local, odd)
    w_attn = gather_rows(lay, attn_rows)
    w_feed_local = pack(
        [gate_weight, up_weight, down_weight],
        [0, hidden_width, 2 * hidden_width],
        3 * hidden_width,
    )
    feed_rows = swap_weight(lay, after(w_feed_local, attn_rows), odd)
    w_feed = gather_rows(lay, feed_rows)
    segment = jnp.where(
        away, lax.ppermute(after(segment_ids, attn_rows), "dp", lay.core), segment_ids
    )
    seg_row = segment[None, :]
    bias = jnp.pad(
        lax.dynamic_slice_in_dim(forget_bias, quarter * heads, heads), (0, 128 - heads)
    )[None, :]

    layer = moved_back(after(layer_input, feed_rows))
    normed = (layer * inverse_rms(layer) * attn_gain).astype(BF)
    xs = gather_pair(lay, normed)
    cot_low = moved(after(output_cotangent.astype(BF), normed))
    cot_z = lax.ppermute(after(cot_low, xs[1]), "tensor", lay.pair)
    attn_normed, qkv, mixed, keep, send, rows, decay, closed = attend(
        place, (*xs[:3], after(xs[3], cot_low)), w_attn, bias, seg_row, heads
    )
    mine, other = scatter_core(lay, keep, after(send, cot_z))
    cot_core = lax.ppermute(after(cot_low, other), "dp", lay.core)
    cot_core_z = lax.ppermute(after(cot_z, other), "dp", lay.core)
    branch = scatter_z(lay, mine, other)
    middle = layer + branch

    feed_local = (middle * inverse_rms(middle) * feed_gain).astype(BF)
    feed_z = lax.ppermute(feed_local, "tensor", lay.pair)
    feed_core = lax.ppermute(feed_local, "dp", lay.core)
    hidden_a, back_a, x_a, c_a, keep_a, send_a = feed(
        (feed_local, feed_core), (cot_low, cot_core), w_feed, 512
    )
    feed_z = after(feed_z, keep_a)
    feed_core_z = lax.ppermute(feed_z, "dp", lay.core)
    hidden_b, back_b, x_b, c_b, keep_b, send_b = feed(
        (feed_z, feed_core_z), (cot_z, cot_core_z), w_feed, 512
    )
    got_a = lax.ppermute(send_a, "dp", lay.core)
    got_b = lax.ppermute(send_b, "dp", lay.core)
    other = (keep_b.astype(F32) + got_b.astype(F32)).astype(BF)
    got_z = lax.ppermute(other, "tensor", lay.pair)
    hidden_b, other = lax.optimization_barrier((hidden_b, other))
    feed_grads = feed_grads_of(
        (x_a, x_b), (c_a, c_b), (back_a, back_b), (hidden_a, hidden_b), 512
    )
    feed_scattered = scatter_rows(lay, feed_grads)
    feed_normed_grad = keep_a.astype(F32) + got_a.astype(F32) + got_z.astype(F32)
    feed_normed_grad = after(feed_normed_grad, feed_grads)

    middle_part = norm_back(middle, feed_gain, feed_normed_grad)
    cotangent = jnp.where(away, cot_low.astype(F32), output_cotangent)
    middle_low = (cotangent + middle_part).astype(BF)
    ms = gather_pair(lay, middle_low)
    down_keep_a, down_send_a, down_keep_b, down_send_b = down_product(
        (hidden_a, after(hidden_b, middle_low)), w_feed
    )
    got_b = lax.ppermute(down_send_b, "dp", lay.core)
    other = (down_keep_b.astype(F32) + got_b.astype(F32)).astype(BF)
    got_a = lax.ppermute(down_send_a, "dp", lay.core)
    ms = (*ms[:3], after(ms[3], other))
    feed_gain_part = sum(
        jnp.sum(part.astype(F32) * x.astype(F32), axis=0)
        for part, x in (
            (after(keep_a, middle_low), x_a[: keep_a.shape[0]]),
            (send_a, x_a[keep_a.shape[0] :]),
            (keep_b, x_b[: keep_b.shape[0]]),
            (send_b, x_b[keep_b.shape[0] :]),
        )
    )
    feed_gain_part = feed_gain_part / feed_gain

    middle_all, grads, keep, send, bias_part = attend_back(
        place, ms, w_attn, qkv, mixed, rows, decay, closed, seg_row, heads
    )
    down = branch + down_keep_a.astype(F32) + got_a.astype(F32)
    down = down + after(lax.ppermute(other, "tensor", lay.pair), bias_part).astype(F32)
    down_back = moved_back(down)
    attn_grads, attn_gain_part = attend_grads(
        place, attn_normed, middle_all, after(grads, down), mixed, keep, send
    )
    layer_output = layer_input + down_back
    bias_full = lax.dynamic_update_slice_in_dim(
        jnp.zeros(forget_bias.shape, F32), bias_part[0, :heads], quarter * heads, 0
    )
    packed = cat(attn_gain_part[0] / attn_gain, feed_gain_part, bias_full)
    size = packed.shape[0]
    packed = jnp.pad(packed, (0, -size % 1024)).reshape(-1, 128)
    small = sum_all(sum_all(packed, "dp"), "tensor")
    attn_scattered = scatter_rows(lay, after(attn_grads, feed_scattered, small, down_back))
    gate_shard, up_shard, down_shard = share_grad(
        lay, after(feed_scattered, small), odd, [hidden_width] * 3
    )
    mine, other = scatter_core(lay, keep, after(send, small))
    attn_normed_grad = scatter_z(lay, mine, other)
    input_part = norm_back(layer, attn_gain, attn_normed_grad)
    input_back = moved_back(after(middle_part + input_part, gate_shard))
    input_grad = output_cotangent + input_back

    small = small.reshape(-1)
    query_shard, key_shard, value_shard, forget_shard, output_shard = share_grad(
        lay,
        after(attn_scattered, small, gate_shard),
        odd,
        [width, width, width, -heads, width],
    )
    return (
        layer_output,
        input_grad,
        small[:features],
        query_shard,
        key_shard,
        value_shard,
        forget_shard.T,
        small[2 * features : size],
        output_shard,
        small[features : 2 * features],
        gate_shard,
        up_shard,
        down_shard,
    )


def solution(mesh):
    tokens = P(("dp", "tensor"), None)
    weight = P("dp", "tensor")
    in_specs = (
        tokens, P("dp"), P(), weight, weight, weight, weight, P(), weight, P(), weight, weight, weight, tokens,
    )
    out_specs = (
        tokens, tokens, P(), weight, weight, weight, weight, P(), weight, P(), weight, weight, weight,
    )
    return jax.shard_map(
        per_device, mesh=mesh, in_specs=in_specs, out_specs=out_specs, check_vma=False
    )
```

```python
import functools

import jax
import jax.numpy as jnp
from jax import lax
from jax.experimental import pallas as pl
from jax.experimental.pallas import tpu as pltpu
from jax.sharding import PartitionSpec as P

F32 = jnp.float32
BF = jnp.bfloat16
NT = (((1,), (1,)), ((), ()))
NN = (((1,), (0,)), ((), ()))
TN = (((0,), (0,)), ((), ()))
BOTH = ("dp", "tensor")
EPS = 1e-6


def dotf(a, b, dn):
    return lax.dot_general(a, b, dn, preferred_element_type=F32)


MIB = 1024 * 1024
VMEM_LIMIT = 60 * MIB


def split3(x):
    a = x.astype(BF)
    r = x - a.astype(F32)
    b = r.astype(BF)
    return a, b, (r - b.astype(F32)).astype(BF)


def exact_dot(left, right, dims):
    return sum(dotf(left, part, dims) for part in split3(right))


def column_of(row):
    parts = [
        jnp.broadcast_to(row[:, i : i + 128], (128, 128)).T[:, :1]
        for i in range(0, row.shape[1], 128)
    ]
    return jnp.concatenate(parts, axis=0)


def starts(place_ref, block):
    odd, zodd = place_ref[0], place_ref[1]
    return [
        pl.multiple_of(
            ((1 - odd if k >> 1 else odd) * 2 + (1 - zodd if k & 1 else zodd)) * block, block
        )
        for k in range(4)
    ]


def attend_kernel(
    heads, span, place_ref, x0_ref, x1_ref, x2_ref, x3_ref, w_ref, bias_ref, seg_ref, x_ref, qkv_ref, mixed_ref, keep_ref, send_ref, rows_ref, decay_ref, closed_ref, stat_ref, drow_ref, own_ref
):
    length = x_ref.shape[0]
    block = length // 4
    width = heads * 64
    places = starts(place_ref, block)
    for at, part_ref in zip(places, (x0_ref, x1_ref, x2_ref, x3_ref)):
        x_ref[pl.ds(at, block), :] = part_ref[...]
    x = x_ref[...]
    qkv_ref[...] = dotf(x, w_ref[:, : 3 * width], NN).astype(BF)
    logits = dotf(x, w_ref[:, 3 * width : 3 * width + 128], NN) + bias_ref[...]
    small = jnp.exp(-jnp.abs(logits))
    log_decay = -(jnp.maximum(-logits, 0.0) + jnp.log1p(small))
    closed_ref[...] = jnp.where(logits >= 0, small, 1.0) / (1.0 + small)
    i = lax.broadcasted_iota(jnp.int32, (128, 128), 0)
    j = lax.broadcasted_iota(jnp.int32, (128, 128), 1)
    below = (i >= j).astype(BF)
    carry = jnp.zeros((1, 128), F32)
    for b in range(0, length, 128):
        total = exact_dot(below, log_decay[b : b + 128], NN) + carry
        decay_ref[b : b + 128, :] = total
        drow_ref[:, b : b + 128] = total.T
        carry = total[127:128]
    lane = lax.broadcasted_iota(jnp.int32, (1, 128), 1)
    i = lax.broadcasted_iota(jnp.int32, (span, span), 0)
    j = lax.broadcasted_iota(jnp.int32, (span, span), 1)
    causal = i >= j
    seg = seg_ref[...]
    for pair in range(heads // 2):
        at = pair * 128
        for begin in range(0, length, span):
            end = begin + span
            q = qkv_ref[begin:end, at : at + 128].astype(F32) * 0.125
            k = qkv_ref[:end, width + at : width + at + 128]
            v = qkv_ref[:end, 2 * width + at : 2 * width + at + 128]
            same = column_of(seg[:, begin:end]) == seg[:, :end]
            outs = []
            for side in range(2):
                h = 2 * pair + side
                own = (lane >= 64) if side else (lane < 64)
                s = dotf(jnp.where(own, q, 0.0).astype(BF), k, NT)
                s = s + decay_ref[begin:end, h : h + 1] - drow_ref[h : h + 1, :end]
                s = jnp.where(same, s, -1e30)
                last = jnp.where(causal, s[:, begin:], -1e30)
                s = jnp.concatenate([s[:, :begin], last], axis=1) if begin else last
                highest = jnp.max(s, axis=1, keepdims=True)
                p = jnp.exp(s - highest)
                total = jnp.sum(p, axis=1, keepdims=True)
                outs.append(dotf(p.astype(BF), v, NN) / total)
                stat_ref[begin:end, h : h + 1] = highest + jnp.log(total)
            mixed_ref[begin:end, at : at + 128] = jnp.where(lane < 64, *outs).astype(BF)
    rows_ref[0:8, :] = drow_ref[0:8, :]
    for b in range(0, length, 128):
        rows_ref[8:16, b : b + 128] = stat_ref[b : b + 128, :].T[0:8]
    for n, at in enumerate(places):
        own_ref[n * block : (n + 1) * block, :] = mixed_ref[pl.ds(at, block), :]
    branch = dotf(own_ref[...], w_ref[:, 3 * width + 128 :], NT)
    keep_ref[...] = branch[: 2 * block].astype(BF)
    send_ref[...] = branch[2 * block :].astype(BF)


def in_memory(scalars, arrays):
    return [pl.BlockSpec(memory_space=pltpu.SMEM)] * scalars + [
        pl.BlockSpec(memory_space=pltpu.VMEM)
    ] * arrays


def attend(place, xs, w, bias, seg, heads):
    block, features = xs[0].shape
    length = 4 * block
    width = heads * 64
    return pl.pallas_call(
        functools.partial(attend_kernel, heads, 256),
        in_specs=in_memory(1, 7),
        out_shape=(
            jax.ShapeDtypeStruct((length, features), BF),
            jax.ShapeDtypeStruct((length, 3 * width), BF),
            jax.ShapeDtypeStruct((length, width), BF),
            jax.ShapeDtypeStruct((length // 2, features), BF),
            jax.ShapeDtypeStruct((length // 2, features), BF),
            jax.ShapeDtypeStruct((16, length), F32),
            jax.ShapeDtypeStruct((length, 128), F32),
            jax.ShapeDtypeStruct((length, 128), F32),
        ),
        scratch_shapes=[
            pltpu.VMEM((length, 128), F32),
            pltpu.VMEM((128, length), F32),
            pltpu.VMEM((length, width), BF),
        ],
        compiler_params=pltpu.CompilerParams(vmem_limit_bytes=38 * MIB),
        cost_estimate=pl.CostEstimate(
            flops=12 * 10**9, bytes_accessed=2 * 10**7, transcendentals=5 * 10**6
        ),
        name="attend",
    )(place, *xs, w, bias, seg)


def attend_back_kernel(
    heads, span, place_ref, m0_ref, m1_ref, m2_ref, m3_ref, w_ref, qkv_ref, mixed_ref, rows_ref, decay_ref, closed_ref, seg_ref, m_ref, grad_ref, keep_ref, send_ref, bias_ref, mb_ref, dq_ref, sums_ref, drow_ref, own_ref
):
    length = m_ref.shape[0]
    block = length // 4
    width = heads * 64
    places = starts(place_ref, block)
    for at, part_ref in zip(places, (m0_ref, m1_ref, m2_ref, m3_ref)):
        m_ref[pl.ds(at, block), :] = part_ref[...]
    mb_ref[...] = dotf(m_ref[...], w_ref[:, 3 * width + 128 :], NN).astype(BF)
    lane = lax.broadcasted_iota(jnp.int32, (1, 128), 1)
    i = lax.broadcasted_iota(jnp.int32, (span, span), 0)
    j = lax.broadcasted_iota(jnp.int32, (span, span), 1)
    causal = i <= j
    seg = seg_ref[...]
    sums_ref[...] = jnp.zeros_like(sums_ref)
    drow_ref[...] = jnp.zeros_like(drow_ref)
    side_row = lax.broadcasted_iota(jnp.int32, (8, 128), 0)
    side_lane = lax.broadcasted_iota(jnp.int32, (8, 128), 1)
    chosen = ((side_lane // 64) == side_row).astype(BF)
    for pair in range(heads // 2):
        at = pair * 128
        own_product = mb_ref[:, at : at + 128].astype(F32) * mixed_ref[:, at : at + 128].astype(F32)
        delta = exact_dot(chosen, own_product, NT)
        for begin in range(0, length, span):
            end = begin + span
            k = qkv_ref[begin:end, width + at : width + at + 128]
            v = qkv_ref[begin:end, 2 * width + at : 2 * width + at + 128]
            q = qkv_ref[begin:, at : at + 128]
            mb = mb_ref[begin:, at : at + 128]
            same = column_of(seg[:, begin:end]) == seg[:, begin:]
            dks, dvs, dqs = [], [], []
            for side in range(2):
                h = 2 * pair + side
                own = (lane >= 64) if side else (lane < 64)
                own_k = jnp.where(own, k.astype(F32) * 0.125, 0.0).astype(BF)
                own_v = jnp.where(own, v.astype(F32), 0.0).astype(BF)
                s = dotf(own_k, q, NT)
                s = s + (rows_ref[h : h + 1, begin:] - rows_ref[8 + h : 9 + h, begin:])
                s = jnp.where(same, s - decay_ref[begin:end, h : h + 1], -1e30)
                first = jnp.where(causal, s[:, :span], -1e30)
                s = jnp.concatenate([first, s[:, span:]], axis=1) if end < length else first
                p = jnp.exp(s)
                dvs.append(dotf(p.astype(BF), mb, NN))
                ds = p * (dotf(own_v, mb, NT) - delta[side : side + 1, begin:])
                ds_low = (ds * 0.125).astype(BF)
                dks.append(dotf(ds_low, q, NN))
                dqs.append(dotf(ds_low, k, TN))
                sums_ref[begin:end, h : h + 1] = jnp.sum(ds, axis=1, keepdims=True)
                drow_ref[h : h + 1, begin:] += jnp.sum(ds, axis=0, keepdims=True)
            k_at, v_at = width + at, 2 * width + at
            grad_ref[begin:end, k_at : k_at + 128] = jnp.where(lane < 64, *dks).astype(BF)
            grad_ref[begin:end, v_at : v_at + 128] = jnp.where(lane < 64, *dvs).astype(BF)
            dq = jnp.where(lane < 64, *dqs)
            if begin:
                dq_ref[begin:, :] += dq
            else:
                dq_ref[...] = dq
        grad_ref[:, at : at + 128] = dq_ref[...].astype(BF)
    i = lax.broadcasted_iota(jnp.int32, (128, 128), 0)
    j = lax.broadcasted_iota(jnp.int32, (128, 128), 1)
    above = (i <= j).astype(BF)
    carry = jnp.zeros((1, 128), F32)
    bias = jnp.zeros((1, 128), F32)
    blank = jnp.zeros((120, 128), F32)
    for b in reversed(range(0, length, 128)):
        row_sum = jnp.concatenate([drow_ref[:, b : b + 128], blank], axis=0).T
        total = exact_dot(above, row_sum - sums_ref[b : b + 128, :], NN) + carry
        carry = total[0:1]
        back = (closed_ref[b : b + 128, :] * total).astype(BF)
        grad_ref[b : b + 128, 3 * width :] = back
        bias = bias + jnp.sum(back.astype(F32), axis=0, keepdims=True)
    bias_ref[...] = jnp.broadcast_to(bias, bias_ref.shape)
    for n, at in enumerate(places):
        own_ref[n * block : (n + 1) * block, :] = grad_ref[pl.ds(at, block), :]
    part = dotf(own_ref[...], w_ref[:, : 3 * width + 128], NT)
    keep_ref[...] = part[: 2 * block].astype(BF)
    send_ref[...] = part[2 * block :].astype(BF)


def attend_back(place, ms, w, qkv, mixed, rows, decay, closed, seg, heads):
    block, features = ms[0].shape
    length = 4 * block
    width = heads * 64
    return pl.pallas_call(
        functools.partial(attend_back_kernel, heads, 256),
        in_specs=in_memory(1, 11),
        out_shape=(
            jax.ShapeDtypeStruct((length, features), BF),
            jax.ShapeDtypeStruct((length, 3 * width + 128), BF),
            jax.ShapeDtypeStruct((length // 2, features), BF),
            jax.ShapeDtypeStruct((length // 2, features), BF),
            jax.ShapeDtypeStruct((8, 128), F32),
        ),
        scratch_shapes=[
            pltpu.VMEM((length, width), BF),
            pltpu.VMEM((length, 128), F32),
            pltpu.VMEM((length, 128), F32),
            pltpu.VMEM((8, length), F32),
            pltpu.VMEM((length, 3 * width + 128), BF),
        ],
        compiler_params=pltpu.CompilerParams(vmem_limit_bytes=38 * MIB),
        cost_estimate=pl.CostEstimate(
            flops=150 * 10**9, bytes_accessed=2 * 10**7, transcendentals=5 * 10**6
        ),
        name="attend_back",
    )(place, *ms, w, qkv, mixed, rows, decay, closed, seg)


def feed_kernel(*refs):
    x_parts, c_parts = refs[:2], refs[2:4]
    wg_ref, wu_ref, wd_ref, hidden_ref, back_ref, x_ref, c_ref, keep_ref, send_ref, total_ref = refs[4:]
    step = pl.program_id(0)
    block = x_ref.shape[0] // 2
    columns = wg_ref.shape[1]

    @pl.when(step == 0)
    def _():
        for n in range(2):
            x_ref[n * block : (n + 1) * block, :] = x_parts[n][...]
            c_ref[n * block : (n + 1) * block, :] = c_parts[n][...]

    x = x_ref[...]
    wg, wu = wg_ref[...], wu_ref[...]
    gate = dotf(x, wg, NN)
    up = dotf(x, wu, NN)
    back = dotf(c_ref[...], wd_ref[...], NN)
    sig = 1.0 / (1.0 + jnp.exp(-gate))
    silu = gate * sig
    hidden_ref[...] = (silu * up).astype(BF)
    back_ref[:, :columns] = (back * up * sig * (1.0 + gate * (1.0 - sig))).astype(BF)
    back_ref[:, columns:] = (back * silu).astype(BF)
    part = dotf(back_ref[...], jnp.concatenate([wg, wu], axis=1), NT)

    @pl.when(step == 0)
    def _():
        total_ref[...] = part

    @pl.when((step > 0) & (step < pl.num_programs(0) - 1))
    def _():
        total_ref[...] += part

    @pl.when(step == pl.num_programs(0) - 1)
    def _():
        keep_ref[...] = (total_ref[:block] + part[:block]).astype(BF)
        send_ref[...] = (total_ref[block:] + part[block:]).astype(BF)


def feed(xs, cs, w, columns):
    rows, features = xs[0].shape
    length = 2 * rows
    width = w.shape[1] // 3
    steps = width // columns
    part = pl.BlockSpec((rows, features), lambda i: (0, 0))
    whole = pl.BlockSpec((length, features), lambda i: (0, 0))
    tall = lambda k: pl.BlockSpec((features, columns), lambda i: (0, i + k * steps))
    return pl.pallas_call(
        feed_kernel,
        grid=(steps,),
        in_specs=[part] * 4 + [tall(0), tall(1), tall(2)],
        out_specs=[
            pl.BlockSpec((length, columns), lambda i: (0, i)),
            pl.BlockSpec((length, 2 * columns), lambda i: (0, i)),
            whole,
            whole,
            part,
            part,
        ],
        out_shape=[
            jax.ShapeDtypeStruct((length, width), BF),
            jax.ShapeDtypeStruct((length, 2 * width), BF),
        ]
        + [jax.ShapeDtypeStruct((length, features), BF)] * 2
        + [jax.ShapeDtypeStruct((rows, features), BF)] * 2,
        scratch_shapes=[pltpu.VMEM((length, features), F32)],
        compiler_params=pltpu.CompilerParams(vmem_limit_bytes=38 * MIB),
        cost_estimate=pl.CostEstimate(
            flops=8 * 10**9, bytes_accessed=18 * 10**6, transcendentals=10**6
        ),
        name="feed",
    )(*xs, *cs, w, w, w)


def feed_grads_kernel(steps, xa_ref, xb_ref, ca_ref, cb_ref, ba_ref, bb_ref, ha_ref, hb_ref, out_ref):
    step = pl.program_id(0)

    @pl.when(step < 2 * steps)
    def _():
        out_ref[...] = (dotf(xa_ref[...], ba_ref[...], TN) + dotf(xb_ref[...], bb_ref[...], TN)).astype(BF)

    @pl.when(step >= 2 * steps)
    def _():
        out_ref[...] = (dotf(ca_ref[...], ha_ref[...], TN) + dotf(cb_ref[...], hb_ref[...], TN)).astype(BF)


def feed_grads_of(xs, cs, backs, hiddens, columns):
    length, features = xs[0].shape
    width = hiddens[0].shape[1]
    steps = width // columns
    whole = pl.BlockSpec((length, features), lambda i: (0, 0))

    def back_at(i):
        i = jnp.minimum(i, 2 * steps - 1)
        return (0, (i % steps) * 2 + i // steps)

    back = pl.BlockSpec((length, columns), back_at)
    hidden = pl.BlockSpec((length, columns), lambda i: (0, jnp.maximum(i - 2 * steps, 0)))
    return pl.pallas_call(
        functools.partial(feed_grads_kernel, steps),
        grid=(3 * steps,),
        in_specs=[whole] * 4 + [back] * 2 + [hidden] * 2,
        out_specs=pl.BlockSpec((features, columns), lambda i: (0, i)),
        out_shape=jax.ShapeDtypeStruct((features, 3 * width), BF),
        compiler_params=pltpu.CompilerParams(vmem_limit_bytes=38 * MIB),
        cost_estimate=pl.CostEstimate(
            flops=12 * length * features * width,
            bytes_accessed=25 * 10**6,
            transcendentals=0,
        ),
        name="feed_grads",
    )(*xs, *cs, *backs, *hiddens)


def down_kernel(ha_ref, hb_ref, w_ref, *outs):
    rows = outs[0].shape[0]
    w = w_ref[...]
    for h_ref, (keep_ref, send_ref) in zip((ha_ref, hb_ref), (outs[:2], outs[2:])):
        part = dotf(h_ref[...], w, NT)
        keep_ref[...] = part[:rows].astype(BF)
        send_ref[...] = part[rows:].astype(BF)


def down_product(hiddens, w):
    length, width = hiddens[0].shape
    features = w.shape[0]
    hidden = pl.BlockSpec((length, width), lambda i: (0, 0))
    part = pl.BlockSpec((length // 2, features), lambda i: (0, 0))
    return pl.pallas_call(
        down_kernel,
        grid=(1,),
        in_specs=[hidden, hidden, pl.BlockSpec((features, width), lambda i: (0, 2))],
        out_specs=[part] * 4,
        out_shape=[jax.ShapeDtypeStruct((length // 2, features), BF)] * 4,
        compiler_params=pltpu.CompilerParams(vmem_limit_bytes=38 * MIB),
        cost_estimate=pl.CostEstimate(
            flops=4 * length * features * width, bytes_accessed=8 * 10**6, transcendentals=0
        ),
        name="down_product",
    )(*hiddens, w)


def unit(rows, columns):
    i = lax.broadcasted_iota(jnp.int32, (rows, columns), 0)
    j = lax.broadcasted_iota(jnp.int32, (rows, columns), 1)
    return (i == j).astype(BF)


def pack_kernel(places, *refs):
    ins, out_ref = refs[:-1], refs[-1]
    for begin, ref in zip(places, ins):
        if ref.shape[0] == out_ref.shape[0]:
            out_ref[:, begin : begin + ref.shape[1]] = ref[...].astype(BF)
        else:
            turned = dotf(ref[...].astype(BF), unit(ref.shape[0], 128), TN)
            out_ref[:, begin : begin + 128] = turned.astype(BF)


def pack(parts, places, columns):
    rows = parts[-1].shape[0]
    return pl.pallas_call(
        functools.partial(pack_kernel, places),
        out_shape=jax.ShapeDtypeStruct((rows, columns), BF),
        compiler_params=pltpu.CompilerParams(vmem_limit_bytes=VMEM_LIMIT),
        cost_estimate=pl.CostEstimate(
            flops=rows * columns, bytes_accessed=6 * rows * columns, transcendentals=0
        ),
        name="pack",
    )(*parts)


def attend_grads_kernel(
    place_ref, x_ref, m_ref, grad_ref, mixed_ref, keep_ref, send_ref, out_ref, gain_ref
):
    inner = grad_ref.shape[1]
    out_ref[:, :inner] = dotf(x_ref[...], grad_ref[...], TN).astype(BF)
    out_ref[:, inner:] = dotf(m_ref[...], mixed_ref[...], TN).astype(BF)
    block = x_ref.shape[0] // 4
    total = jnp.zeros((1, gain_ref.shape[1]), F32)
    for n, at in enumerate(starts(place_ref, block)):
        part = (send_ref if n >> 1 else keep_ref)[(n & 1) * block : ((n & 1) + 1) * block, :]
        own = x_ref[pl.ds(at, block), :].astype(F32) * part.astype(F32)
        total = total + jnp.sum(own, axis=0, keepdims=True)
    gain_ref[...] = jnp.broadcast_to(total, gain_ref.shape)


def attend_grads(place, x, m, grads, mixed, keep, send):
    length, features = x.shape
    columns = grads.shape[1] + mixed.shape[1]
    return pl.pallas_call(
        attend_grads_kernel,
        in_specs=in_memory(1, 6),
        out_shape=(
            jax.ShapeDtypeStruct((features, columns), BF),
            jax.ShapeDtypeStruct((8, features), F32),
        ),
        compiler_params=pltpu.CompilerParams(vmem_limit_bytes=38 * MIB),
        cost_estimate=pl.CostEstimate(
            flops=2 * length * features * columns, bytes_accessed=2 * 10**7, transcendentals=0
        ),
        name="attend_grads",
    )(place, x, m, grads, mixed, keep, send)


def finish_kernel(widths, odd_ref, low_ref, high_ref, a_ref, b_ref, c_ref, *out_refs):
    odd = odd_ref[0] == 1

    def put(first_ref, second_ref):
        begin = 0
        for width, out_ref in zip(widths, out_refs):
            if width > 0:
                first = first_ref[:, begin : begin + width].astype(F32)
                out_ref[...] = first + second_ref[:, begin : begin + width].astype(F32)
            else:
                width = 128
                pick = unit(out_ref.shape[0], 128)
                out_ref[...] = dotf(pick, first_ref[:, begin : begin + 128], NT) + dotf(
                    pick, second_ref[:, begin : begin + 128], NT
                )
            begin += width

    @pl.when(odd)
    def _():
        put(c_ref, b_ref)

    @pl.when(jnp.logical_not(odd))
    def _():
        put(low_ref, a_ref)


def finish(odd, low, high, a, b, c, widths):
    rows = low.shape[0]
    return pl.pallas_call(
        functools.partial(finish_kernel, widths),
        in_specs=in_memory(1, 5),
        out_shape=[
            jax.ShapeDtypeStruct((rows, width) if width > 0 else (-width, rows), F32)
            for width in widths
        ],
        compiler_params=pltpu.CompilerParams(vmem_limit_bytes=38 * MIB),
        cost_estimate=pl.CostEstimate(flops=10**6, bytes_accessed=8 * 10**6, transcendentals=0),
        name="finish",
    )(odd, low, high, a, b, c)


class Layout:
    def __init__(self, dp, tensor):
        self.groups = [[core + 2 * i for i in range(dp // 2)] for core in range(2)]
        self.core = [(d, d ^ 1) for d in range(dp)]
        self.pair = [(z, z ^ 1) for z in range(tensor)]
        flat = lambda d, z: d * tensor + z
        devices = [(d, z) for d in range(dp) for z in range(tensor)]
        away = [(d, z) for d, z in devices if (d & 1) != (z >> 1)]
        self.move = [(flat(d, z), flat(d ^ 1, z ^ 2)) for d, z in away]
        even = [(d, z) for d, z in devices if d & 1 == 0]
        odd = [(d, z) for d, z in devices if d & 1 == 1]
        self.even_far = [(flat(d, z), flat(d + 1, z ^ 2)) for d, z in even]
        self.odd_far = [(flat(d, z), flat(d, z ^ 2)) for d, z in odd]
        self.odd_even = [(flat(d, z), flat(d - 1, z)) for d, z in odd]
        self.back_even_far = [(b, a) for a, b in self.even_far]
        self.back_odd_even = [(b, a) for a, b in self.odd_even]


def cat(*parts):
    return jnp.concatenate(parts, axis=0)


def after(x, *deps):
    return lax.optimization_barrier((x, *deps))[0]


def swap_weight(lay, w, odd, *deps):
    a = lax.ppermute(w, BOTH, lay.even_far)
    b = lax.ppermute(w, BOTH, lay.odd_far)
    c = lax.ppermute(w, BOTH, lay.odd_even)
    return jnp.where(odd, cat(after(a, *deps), b), cat(w, c))


def gather_rows(lay, rows):
    return lax.all_gather(rows, "dp", axis=0, tiled=True, axis_index_groups=lay.groups)


def scatter_rows(lay, g):
    return lax.psum_scatter(
        g, "dp", scatter_dimension=0, tiled=True, axis_index_groups=lay.groups
    )


def share_grad(lay, r, odd, widths):
    half = r.shape[0] // 2
    low, high = r[:half], r[half:]
    a = lax.ppermute(low, BOTH, lay.back_even_far)
    b = lax.ppermute(high, BOTH, lay.odd_far)
    c = lax.ppermute(high, BOTH, lay.back_odd_even)
    return finish(odd.astype(jnp.int32).reshape(1), low, high, a, b, c, widths)


def gather_pair(lay, x, *deps):
    core = lax.ppermute(x, "dp", lay.core)
    z = lax.ppermute(x, "tensor", lay.pair)
    return x, z, core, lax.ppermute(after(z, *deps), "dp", lay.core)


def scatter_core(lay, keep, send):
    got = lax.ppermute(send, "dp", lay.core)
    half = keep.shape[0] // 2
    mine = keep[:half].astype(F32) + got[:half].astype(F32)
    other = keep[half:].astype(F32) + got[half:].astype(F32)
    return mine, other.astype(BF)


def scatter_z(lay, mine, other):
    return mine + lax.ppermute(other, "tensor", lay.pair).astype(F32)


def sum_all(x, axis):
    size = lax.axis_size(axis)
    step = 1
    while step < size:
        x = x + lax.ppermute(x, axis, [(i, i ^ step) for i in range(size)])
        step *= 2
    return x


def inverse_rms(rows):
    return lax.rsqrt(jnp.mean(rows * rows, axis=-1, keepdims=True) + EPS)


def norm_back(rows, gain, grad):
    r = inverse_rms(rows)
    xhat = rows * r
    scaled = grad * gain
    return r * (scaled - xhat * jnp.mean(scaled * xhat, axis=-1, keepdims=True))


def per_device(
    layer_input,
    segment_ids,
    attn_gain,
    query_weight,
    key_weight,
    value_weight,
    forget_weight,
    forget_bias,
    output_weight,
    feed_gain,
    gate_weight,
    up_weight,
    down_weight,
    output_cotangent,
):
    lay = Layout(lax.axis_size("dp"), lax.axis_size("tensor"))
    z = lax.axis_index("tensor")
    odd = (lax.axis_index("dp") & 1) == 1
    zodd = (z & 1) == 1
    away = odd != (z >= 2)
    quarter = jnp.where(odd, z ^ 2, z)
    heads = forget_weight.shape[1]
    width = query_weight.shape[1]
    hidden_width = gate_weight.shape[1]
    features = layer_input.shape[1]
    place = jnp.stack([odd, zodd]).astype(jnp.int32)

    def moved(x):
        return jnp.where(away, lax.ppermute(x, BOTH, lay.move), x)

    def moved_back(x):
        low = lax.ppermute(x.astype(BF), BOTH, lay.move)
        return jnp.where(away, low.astype(F32), x)

    w_attn_local = pack(
        [query_weight, key_weight, value_weight, forget_weight.T, output_weight],
        [0, width, 2 * width, 3 * width, 3 * width + 128],
        4 * width + 128,
    )
    attn_rows = swap_weight(lay, w_attn_local, odd)
    w_attn = gather_rows(lay, attn_rows)
    w_feed_local = pack(
        [gate_weight, up_weight, down_weight],
        [0, hidden_width, 2 * hidden_width],
        3 * hidden_width,
    )
    feed_rows = swap_weight(lay, after(w_feed_local, attn_rows), odd)
    w_feed = gather_rows(lay, feed_rows)
    segment = jnp.where(
        away, lax.ppermute(after(segment_ids, attn_rows), "dp", lay.core), segment_ids
    )
    seg_row = segment[None, :]
    bias = jnp.pad(
        lax.dynamic_slice_in_dim(forget_bias, quarter * heads, heads), (0, 128 - heads)
    )[None, :]

    layer = moved_back(after(layer_input, feed_rows))
    normed = (layer * inverse_rms(layer) * attn_gain).astype(BF)
    xs = gather_pair(lay, normed)
    cot_low = moved(after(output_cotangent.astype(BF), normed))
    cot_z = lax.ppermute(after(cot_low, xs[1]), "tensor", lay.pair)
    attn_normed, qkv, mixed, keep, send, rows, decay, closed = attend(
        place, (*xs[:3], after(xs[3], cot_low)), w_attn, bias, seg_row, heads
    )
    mine, other = scatter_core(lay, keep, after(send, cot_z))
    cot_core = lax.ppermute(after(cot_low, other), "dp", lay.core)
    cot_core_z = lax.ppermute(after(cot_z, other), "dp", lay.core)
    branch = scatter_z(lay, mine, other)
    middle = layer + branch

    feed_local = (middle * inverse_rms(middle) * feed_gain).astype(BF)
    feed_z = lax.ppermute(feed_local, "tensor", lay.pair)
    feed_core = lax.ppermute(feed_local, "dp", lay.core)
    hidden_a, back_a, x_a, c_a, keep_a, send_a = feed(
        (feed_local, feed_core), (cot_low, cot_core), w_feed, 512
    )
    feed_z = after(feed_z, keep_a)
    feed_core_z = lax.ppermute(feed_z, "dp", lay.core)
    hidden_b, back_b, x_b, c_b, keep_b, send_b = feed(
        (feed_z, feed_core_z), (cot_z, cot_core_z), w_feed, 512
    )
    got_a = lax.ppermute(send_a, "dp", lay.core)
    got_b = lax.ppermute(send_b, "dp", lay.core)
    other = (keep_b.astype(F32) + got_b.astype(F32)).astype(BF)
    got_z = lax.ppermute(other, "tensor", lay.pair)
    hidden_b, other = lax.optimization_barrier((hidden_b, other))
    feed_grads = feed_grads_of(
        (x_a, x_b), (c_a, c_b), (back_a, back_b), (hidden_a, hidden_b), 512
    )
    feed_scattered = scatter_rows(lay, feed_grads)
    feed_normed_grad = keep_a.astype(F32) + got_a.astype(F32) + got_z.astype(F32)
    feed_normed_grad = after(feed_normed_grad, feed_grads)

    middle_part = norm_back(middle, feed_gain, feed_normed_grad)
    cotangent = jnp.where(away, cot_low.astype(F32), output_cotangent)
    middle_low = (cotangent + middle_part).astype(BF)
    ms = gather_pair(lay, middle_low)
    down_keep_a, down_send_a, down_keep_b, down_send_b = down_product(
        (hidden_a, after(hidden_b, middle_low)), w_feed
    )
    got_b = lax.ppermute(down_send_b, "dp", lay.core)
    other = (down_keep_b.astype(F32) + got_b.astype(F32)).astype(BF)
    got_a = lax.ppermute(down_send_a, "dp", lay.core)
    ms = (*ms[:3], after(ms[3], other))
    feed_gain_part = sum(
        jnp.sum(part.astype(F32) * x.astype(F32), axis=0)
        for part, x in (
            (after(keep_a, middle_low), x_a[: keep_a.shape[0]]),
            (send_a, x_a[keep_a.shape[0] :]),
            (keep_b, x_b[: keep_b.shape[0]]),
            (send_b, x_b[keep_b.shape[0] :]),
        )
    )
    feed_gain_part = feed_gain_part / feed_gain

    middle_all, grads, keep, send, bias_part = attend_back(
        place, ms, w_attn, qkv, mixed, rows, decay, closed, seg_row, heads
    )
    down = branch + down_keep_a.astype(F32) + got_a.astype(F32)
    down = down + after(lax.ppermute(other, "tensor", lay.pair), bias_part).astype(F32)
    down_back = moved_back(down)
    attn_grads, attn_gain_part = attend_grads(
        place, attn_normed, middle_all, after(grads, down), mixed, keep, send
    )
    layer_output = layer_input + down_back
    bias_full = lax.dynamic_update_slice_in_dim(
        jnp.zeros(forget_bias.shape, F32), bias_part[0, :heads], quarter * heads, 0
    )
    packed = cat(attn_gain_part[0] / attn_gain, feed_gain_part, bias_full)
    size = packed.shape[0]
    packed = jnp.pad(packed, (0, -size % 1024)).reshape(-1, 128)
    small = sum_all(sum_all(packed, "dp"), "tensor")
    attn_scattered = scatter_rows(lay, after(attn_grads, feed_scattered, down_back))
    gate_shard, up_shard, down_shard = share_grad(
        lay, after(feed_scattered, small), odd, [hidden_width] * 3
    )
    mine, other = scatter_core(lay, keep, after(send, small))
    attn_normed_grad = scatter_z(lay, mine, other)
    input_part = norm_back(layer, attn_gain, attn_normed_grad)
    input_back = moved_back(after(middle_part + input_part, gate_shard))
    input_grad = output_cotangent + input_back

    small = small.reshape(-1)
    query_shard, key_shard, value_shard, forget_shard, output_shard = share_grad(
        lay,
        after(attn_scattered, small, gate_shard),
        odd,
        [width, width, width, -heads, width],
    )
    return (
        layer_output,
        input_grad,
        small[:features],
        query_shard,
        key_shard,
        value_shard,
        forget_shard.T,
        small[2 * features : size],
        output_shard,
        small[features : 2 * features],
        gate_shard,
        up_shard,
        down_shard,
    )


def solution(mesh):
    tokens = P(("dp", "tensor"), None)
    weight = P("dp", "tensor")
    in_specs = (
        tokens, P("dp"), P(), weight, weight, weight, weight, P(), weight, P(), weight, weight, weight, tokens,
    )
    out_specs = (
        tokens, tokens, P(), weight, weight, weight, weight, P(), weight, P(), weight, weight, weight,
    )
    return jax.shard_map(
        per_device, mesh=mesh, in_specs=in_specs, out_specs=out_specs, check_vma=False
    )
```
